256 devices in a mesh: path: 16 (over z_hi, y, core), fsdp: 16 (over x, z_lo).
Axes of the slice: x: 4, y: 4, z: 8 (z_hi: 2, z_lo: 4; z = z_hi * 4 + z_lo), core: 2. Of those that a mesh axis runs over, the one named last changes fastest.
Arguments:
- inputs: bfloat16 [16, 2048, 2048], P('path', 'fsdp'), may hold values from -6 to 6
- targets: bfloat16 [16, 2048, 2048], P('path', 'fsdp'), may hold values from -6 to 6
- token_ids: int32 [16, 2048], P('path', 'fsdp'), may hold values from 0 to 31999, as said below
- module_table: int32 [16, 2], replicated, may hold values from 0 to 3, as said below
- path_weights: bfloat16 [16, 2, 2048, 5632], P('path', None, None, 'fsdp'), may hold values from -6 to 6
- master: float32 [2, 4, 2048, 5632], P(None, None, 'path', 'fsdp'), may hold values from -6 to 6
- momentum: float32 [2, 4, 2048, 5632], P(None, None, 'path', 'fsdp'), may hold values from -6 to 6
Outputs:
- new_weights: bfloat16 [16, 2, 2048, 5632], P('path', None, None, 'fsdp')
- new_master: float32 [2, 4, 2048, 5632], P(None, None, 'path', 'fsdp')
- new_momentum: float32 [2, 4, 2048, 5632], P(None, None, 'path', 'fsdp')
The draws below stay inside these ranges and needn't reach their ends.
Inputs may be any that keep to these rules, and one draw needn't show every extreme that they name: `module_table`: at each level, every module is named by exactly 4 paths. `token_ids`: ids below 256 are control tokens.
All inputs are finite; a program needn't handle non-finite values.
Results may differ from the reference program's by a relative error of at most 0.014.
Values may be sent and summed in bfloat16 or wider, within the bound.
A program may use at most 128 MiB of HBM per device.

```python
import jax
import jax.numpy as jnp
from jax import lax

D = 2048
FF = 5632
VOCAB = 32000
SPECIAL = 256
MODS = 4
LEVELS = 2
PATHS = 16
TOKENS = 2048
N_FSDP = 16


def draw_token_ids(key, part):
    key = jax.random.fold_in(key, 11)
    k_kind, k_control, k_text, k_spots = jax.random.split(key, 4)
    kind = jax.random.randint(k_kind, (PATHS, TOKENS), 0, 3)
    control = jax.random.randint(k_control, (PATHS, TOKENS), 0, SPECIAL)
    text = jax.random.randint(k_text, (PATHS, TOKENS), SPECIAL, VOCAB)
    drawn = jnp.where(kind == 0, control, text)
    spots = jax.random.randint(k_spots, (2,), 0, PATHS * TOKENS)
    flat_pos = jnp.arange(PATHS * TOKENS, dtype=jnp.int32).reshape(PATHS, TOKENS)
    drawn = jnp.where(flat_pos == spots[0], VOCAB - 1, drawn)
    drawn = jnp.where(flat_pos == spots[1], 0, drawn)
    return drawn.astype(jnp.int32)


def draw_module_table(key, part):
    key = jax.random.fold_in(key, 23)
    columns = []
    for level in range(LEVELS):
        order = jax.random.permutation(jax.random.fold_in(key, level), PATHS)
        columns.append(order % MODS)
    return jnp.stack(columns, axis=1).astype(jnp.int32)


def level_of(rng, extent, cuts, smallest, largest):
    factor_of, own = 1.0, jax.random.fold_in(rng, 6)
    for dim, parts in cuts:
        draws = jnp.exp(jax.random.uniform(jax.random.fold_in(own, dim), (parts,), jnp.float32, smallest / len(cuts), largest / len(cuts)))
        factor_of = factor_of * jnp.repeat(draws, extent[dim] // parts).reshape([-1 if axis == dim else 1 for axis in range(len(extent))])
    return factor_of


def normal_values(own_key, shape, scale, bound, cuts=(), kind=jnp.bfloat16):
    result = scale * jax.random.normal(own_key, shape, jnp.float32)
    if cuts:
        result = result * level_of(own_key, shape, cuts, -0.22, 0.18)
    return jnp.clip(result, -bound, bound).astype(kind)


def setup_inputs(seed: int = 0) -> dict:
    splits = jax.random.split(jax.random.key(seed), 8)
    return {
        "inputs": normal_values(splits[0], (PATHS, TOKENS, D), 1.0, 6.0, ((0, 16), (1, 16))),
        "targets": normal_values(splits[1], (PATHS, TOKENS, D), 1.0, 6.0, ((0, 16), (1, 16))),
        "token_ids": draw_token_ids(jax.random.fold_in(splits[7], 71), 0),
        "module_table": draw_module_table(jax.random.fold_in(splits[7], 71), 0),
        "path_weights": normal_values(splits[4], (PATHS, LEVELS, D, FF), 1.0, 6.0, ((0, 16), (3, 16))),
        "master": normal_values(splits[5], (LEVELS, MODS, D, FF), 1.0, 6.0, ((2, 16), (3, 16)), jnp.float32),
        "momentum": normal_values(splits[6], (LEVELS, MODS, D, FF), 1.0, 6.0, ((2, 16), (3, 16)), jnp.float32),
    }


INNER_LR = 4096.0
OUTER_LR = 0.7
MOMENT = 0.9


def path_delta(x_rows, tgt_rows, ids, w_in, w_out):
    piece = FF // N_FSDP
    pre = jnp.dot(x_rows, w_in, preferred_element_type=jnp.float32) * (D ** -0.5)
    sig = jax.nn.sigmoid(pre)
    act = (pre * sig).astype(jnp.bfloat16)

    def add_block(total, block):
        start = (block * piece).astype(jnp.int32)
        a_part = lax.dynamic_slice_in_dim(act, start, piece, 1)
        w_part = lax.dynamic_slice_in_dim(w_out, start, piece, 1)
        term = lax.dot_general(a_part, w_part, (((1,), (1,)), ((), ())), preferred_element_type=jnp.float32) * (FF ** -0.5)
        rounded = lax.optimization_barrier(term.astype(jnp.bfloat16))
        return total + rounded.astype(jnp.float32), None

    mixed, _ = lax.scan(add_block, jnp.zeros((TOKENS, D), jnp.float32), jnp.arange(N_FSDP, dtype=jnp.int32))
    keep = (ids >= SPECIAL).astype(jnp.float32)
    out_grad = (keep[:, None] * (x_rows.astype(jnp.float32) + mixed - tgt_rows.astype(jnp.float32)) / TOKENS).astype(jnp.bfloat16)
    act_grad = jnp.dot(out_grad, w_out, preferred_element_type=jnp.float32) * (FF ** -0.5)
    pre_grad = (act_grad * sig * (1.0 + pre * (1.0 - sig))).astype(jnp.bfloat16)
    grad_out = lax.dot_general(out_grad, act, (((0,), (0,)), ((), ())), preferred_element_type=jnp.float32) * (FF ** -0.5)
    grad_in = lax.dot_general(x_rows, pre_grad, (((0,), (0,)), ((), ())), preferred_element_type=jnp.float32) * (D ** -0.5)
    return jnp.stack([INNER_LR * grad_in, INNER_LR * grad_out])


def reference(inputs, targets, token_ids, module_table, path_weights, master, momentum):
    labels = jnp.arange(MODS, dtype=jnp.int32)

    def add_path(sums, index):
        delta = path_delta(inputs[index], targets[index], token_ids[index], path_weights[index, 0], path_weights[index, 1])
        pick = (module_table[index][:, None] == labels[None, :]).astype(jnp.float32)
        return sums + pick[:, :, None, None] * delta[:, None], None

    sums, _ = lax.scan(add_path, jnp.zeros((LEVELS, MODS, D, FF), jnp.float32), jnp.arange(PATHS, dtype=jnp.int32))
    counts = jnp.sum((module_table.T[:, :, None] == labels[None, None, :]).astype(jnp.float32), axis=1)
    average = sums / counts[:, :, None, None]
    new_momentum = MOMENT * momentum + average
    new_master = master - OUTER_LR * (average + MOMENT * new_momentum)
    fresh = new_master.astype(jnp.bfloat16)
    levels = [jnp.take(fresh[level], module_table[:, level], axis=0) for level in range(LEVELS)]
    new_weights = jnp.stack(levels, axis=1)
    return new_weights, new_master, new_momentum
```

```python
import functools

import jax
import jax.numpy as jnp
from jax import lax
from jax.experimental import pallas as pl
from jax.experimental.pallas import tpu as pltpu
from jax.sharding import PartitionSpec as P

SPECIAL = 256
INNER_LR = 4096.0
OUTER_LR = 0.7
MOMENT = 0.9
MESH = pl.DeviceIdType.MESH

RA, RB = 96, 32
HA, HB = RA // 2, RB // 2
NX, NZ = 4, 4
ROWS_A = NX * NZ * RA
SUPER = NX * RB


class Place:
    def __init__(self):
        f = lax.axis_index("fsdp")
        self.x, self.z = f // NZ, f % NZ
        self.far = self.z // 2
        self.w = (self.z + self.far) % 2
        flip = 1 - 2 * self.far
        self.flip = flip
        self.right = ((self.x + 1) % NX) * NZ + self.z
        self.left = ((self.x + NX - 1) % NX) * NZ + self.z
        self.inner = self.x * NZ + self.z + flip
        self.edge = self.x * NZ + self.z - flip

    def zb(self, r):
        swap = jnp.where(r == 0, 1, jnp.where(r == 1, -1, 0))
        o = r + self.w * swap
        return o * self.flip + (NZ - 1) * self.far

    def col(self, dx):
        return (self.x + dx + NX) % NX


def rows_a(x, z):
    return pl.multiple_of((x * NZ + z) * RA, 16)


def rows_b(x, z):
    return pl.multiple_of(ROWS_A + (z * NX + x) * RB, 16)


def rows_super(z):
    return pl.multiple_of(ROWS_A + z * SUPER, 16)


def rcopy(src, dst, ssem, rsem, f):
    return pltpu.make_async_remote_copy(
        src_ref=src, dst_ref=dst, send_sem=ssem, recv_sem=rsem, device_id={"fsdp": f}, device_id_type=MESH
    )


def gather(pp, buf, ssem, rsem, compute):
    x, z, w = pp.x, pp.z, pp.w

    def piece(start, n):
        return buf.at[pl.ds(start, n)]

    def push(kind, side, i, start, n, f, slot):
        rcopy(piece(start, n), piece(start, n), ssem.at[kind, side, i], rsem.at[kind, slot[0], slot[1]], f).start()

    def arrived(kind, side, i, start, n):
        rcopy(piece(start, n), piece(start, n), ssem.at[kind, side, i], rsem.at[kind, side, i], pp.right).wait_recv()

    def sent(kind, side, i, n):
        rcopy(piece(0, n), piece(0, n), ssem.at[kind, side, i], rsem.at[kind, side, i], pp.right).wait_send()

    own_a, own_b = rows_a(x, z), rows_b(x, z)

    def z_own(kind, start, n):
        push(kind, 0, 0, start, n, pp.inner, (0, z))

        @pl.when(w == 1)
        def _():
            push(kind, 1, 0, start, n, pp.edge, (0, z))

    def z_forward(kind, r, zb, start, n):
        @pl.when((w == 1) & (r == 1))
        def _():
            push(kind, 0, r, start, n, pp.inner, (0, zb))

        @pl.when((w == 1) & (r >= 2))
        def _():
            push(kind, 1, r, start, n, pp.edge, (0, zb))

    z_own(0, own_a, RA)
    for side, f in ((0, pp.right), (1, pp.left)):
        push(3, side, 0, own_b, RB, f, (side, 0))

    def step(t, carry):
        zt = pp.zb(t)
        col_t = rows_a(x, zt)

        @pl.when((t >= 1) & (t <= 3))
        def _():
            arrived(0, 0, zt, col_t, RA)
            z_forward(0, t, zt, col_t, RA)

        @pl.when(t <= 3)
        def _():
            for side, f in ((0, pp.right), (1, pp.left)):
                push(1, side, t, col_t, RA, f, (side, t))

        @pl.when(t == 0)
        def _():
            for side, dx, f in ((0, -1, pp.right), (1, 1, pp.left)):
                start = rows_b(pp.col(dx), z)
                arrived(3, side, 0, start, RB)
                push(4, side, 0, pl.multiple_of(start + side * HB, 16), HB, f, (side, 0))

        zl = pp.zb(t - 1)

        @pl.when((t >= 1) & (t <= 4))
        def _():
            for side, dx, f in ((0, -1, pp.right), (1, 1, pp.left)):
                start = rows_a(pp.col(dx), zl)
                arrived(1, side, t - 1, start, RA)
                push(2, side, t - 1, pl.multiple_of(start + side * HA, 16), HA, f, (side, t - 1))

        @pl.when(t == 1)
        def _():
            start = rows_b(pp.col(2), z)
            for side in (0, 1):
                arrived(4, side, 0, pl.multiple_of(start + side * HB, 16), HB)
            z_own(5, rows_super(z), SUPER)

        @pl.when((t >= 2) & (t <= 4))
        def _():
            arrived(5, 0, zl, rows_super(zl), SUPER)
            z_forward(5, t - 1, zl, rows_super(zl), SUPER)

        @pl.when(t <= 3)
        def _():
            compute(col_t, RA)

        @pl.when((t >= 1) & (t <= 4))
        def _():
            def sides(j, c):
                compute(rows_a(pp.col(2 * j - 1), zl), RA)
                return c

            lax.fori_loop(0, 2, sides, 0)
            compute(rows_super(zl), SUPER)

        @pl.when(t >= 2)
        def _():
            start = rows_a(pp.col(2), pp.zb(t - 2))
            for side in (0, 1):
                arrived(2, side, t - 2, pl.multiple_of(start + side * HA, 16), HA)
            compute(start, RA)

        return carry

    lax.fori_loop(0, 6, step, 0)

    for kind, n in ((0, RA), (5, SUPER)):
        sent(kind, 0, 0, n)

        @pl.when(w == 1)
        def _():
            sent(kind, 1, 0, n)
            sent(kind, 0, 1, n)
            sent(kind, 1, 2, n)
            sent(kind, 1, 3, n)

    for side in (0, 1):
        sent(3, side, 0, RB)
        sent(4, side, 0, HB)

        def drain(i, c):
            sent(1, side, i, RA)
            sent(2, side, i, HA)
            return c

        lax.fori_loop(0, 4, drain, 0)


COLS = 512


def reduce(pp, partial, sc):
    x, z, w = pp.x, pp.z, pp.w
    width = sc.acc_a.shape[1]
    ssem, rsem = sc.rs_send, sc.rs_recv

    def chunks(body):
        def run(k, c):
            body(pl.ds(pl.multiple_of(k * COLS, 128), COLS))
            return c

        lax.fori_loop(0, width // COLS, run, 0)

    def push(src, dst, kind, side, i, f, slot):
        rcopy(src, dst, ssem.at[kind, side, i], rsem.at[kind, slot[0], slot[1]], f).start()

    def arrived(ref, kind, side, i):
        rcopy(ref, ref, ssem.at[kind, side, i], rsem.at[kind, side, i], pp.right).wait_recv()

    def sent(ref, kind, side, i):
        rcopy(ref, ref, ssem.at[kind, side, i], rsem.at[kind, side, i], pp.right).wait_send()

    def up(v):
        return v.astype(jnp.float32)

    def z_stage(kind, r, acc, recv, send):
        @pl.when((w == 1) & (r >= 1))
        def _():
            arrived(recv.at[r], kind, 0, r)

            def add(cs):
                send[r, :, cs] = (acc[:, cs] + up(recv[r, :, cs])).astype(jnp.bfloat16)

            chunks(add)

        @pl.when((w == 1) & (r >= 2))
        def _():
            slot = jnp.where(r == 3, 1, 0)
            push(send.at[r], recv.at[slot], kind, 0, r, pp.inner, (0, slot))

        @pl.when((w == 1) & (r == 1))
        def _():
            push(send.at[r], recv.at[0], kind, 0, r, pp.edge, (0, 0))

        @pl.when((w == 0) & (r >= 1))
        def _():
            def cast(cs):
                send[r, :, cs] = acc[:, cs].astype(jnp.bfloat16)

            chunks(cast)
            slot = jnp.where(r == 1, 4, r)
            push(send.at[r], recv.at[slot], kind, 0, r, pp.inner, (0, slot))

        @pl.when(r == 0)
        def _():
            arrived(recv.at[0], kind, 0, 0)

            def add(cs):
                acc[:, cs] = acc[:, cs] + up(recv[0, :, cs])

            chunks(add)

        @pl.when((w == 1) & (r == 0))
        def _():
            arrived(recv.at[4], kind, 0, 4)

            def add(cs):
                acc[:, cs] = acc[:, cs] + up(recv[4, :, cs])

            chunks(add)

    def b_round(r):
        start = rows_super(pp.zb(r))

        def fill(cs):
            sc.acc_b[:, cs] = partial(start, SUPER, cs)

        chunks(fill)
        z_stage(4, r, sc.acc_b, sc.b_recv, sc.b_send)

    def step(t, carry):
        r0, r1, r2 = 3 - t, 4 - t, 5 - t

        @pl.when(t <= 3)
        def _():
            start = rows_a(pp.col(2), pp.zb(r0))

            def fill(cs):
                sc.h_send[r0, :, cs] = partial(start, RA, cs).astype(jnp.bfloat16)

            chunks(fill)
            push(sc.h_send.at[r0, pl.ds(0, HA)], sc.h_recv.at[1, r0], 0, 1, r0, pp.left, (1, r0))
            push(sc.h_send.at[r0, pl.ds(HA, HA)], sc.h_recv.at[0, r0], 0, 0, r0, pp.right, (0, r0))

        @pl.when((t == 0) & (w == 0))
        def _():
            def run(i, c):
                b_round(3 - i)
                return c

            lax.fori_loop(0, 3, run, 0)

        @pl.when((t >= 1) & (t <= 4))
        def _():
            zr = pp.zb(r1)
            for side, dx, f, lo in ((0, 1, pp.right, HA), (1, -1, pp.left, 0)):
                start = rows_a(pp.col(dx), zr)
                arrived(sc.h_recv.at[side, r1], 0, side, r1)

                def fill(cs):
                    part = partial(start, RA, cs)
                    got = up(sc.h_recv[side, r1, :, cs])
                    both = part[lo : lo + HA] + got
                    alone = part[HA - lo : HA - lo + HA]
                    sc.f_send[side, r1, pl.ds(lo, HA), cs] = both.astype(jnp.bfloat16)
                    sc.f_send[side, r1, pl.ds(HA - lo, HA), cs] = alone.astype(jnp.bfloat16)

                chunks(fill)
                push(sc.f_send.at[side, r1], sc.f_recv.at[side, r1], 1, side, r1, f, (side, r1))

        @pl.when((t >= 1) & (t <= 3) & (w == 1))
        def _():
            b_round(r1)

        @pl.when(t == 4)
        def _():
            b_round(0)
            start = pl.multiple_of(pp.col(2) * RB, RB)
            sc.bh_send[...] = sc.acc_b[pl.ds(start, RB), :].astype(jnp.bfloat16)
            push(sc.bh_send.at[pl.ds(0, HB)], sc.bh_recv.at[1], 2, 1, 0, pp.left, (1, 0))
            push(sc.bh_send.at[pl.ds(HB, HB)], sc.bh_recv.at[0], 2, 0, 0, pp.right, (0, 0))

        @pl.when(t >= 2)
        def _():
            start = rows_a(x, pp.zb(r2))
            for side in (0, 1):
                arrived(sc.f_recv.at[side, r2], 1, side, r2)

            def fill(cs):
                sc.acc_a[:, cs] = partial(start, RA, cs) + up(sc.f_recv[0, r2, :, cs]) + up(sc.f_recv[1, r2, :, cs])

            chunks(fill)
            z_stage(3, r2, sc.acc_a, sc.a_recv, sc.a_send)

        @pl.when(t == 4)
        def _():
            for side, dx, f, lo in ((0, 1, pp.right, HB), (1, -1, pp.left, 0)):
                start = pl.multiple_of(pp.col(dx) * RB, RB)
                arrived(sc.bh_recv.at[side], 2, side, 0)

                def fill(cs):
                    got = up(sc.bh_recv[side, :, cs])
                    both = sc.acc_b[pl.ds(pl.multiple_of(start + lo, 8), HB), cs] + got
                    alone = sc.acc_b[pl.ds(pl.multiple_of(start + HB - lo, 8), HB), cs]
                    sc.bf_send[side, pl.ds(lo, HB), cs] = both.astype(jnp.bfloat16)
                    sc.bf_send[side, pl.ds(HB - lo, HB), cs] = alone.astype(jnp.bfloat16)

                chunks(fill)
                push(sc.bf_send.at[side], sc.bf_recv.at[side], 5, side, 0, f, (side, 0))

        return carry

    lax.fori_loop(0, 6, step, 0)
    for side in (0, 1):
        arrived(sc.bf_recv.at[side], 5, side, 0)
    own = pl.multiple_of(x * RB, RB)

    def last(cs):
        sc.fin_b[:, cs] = sc.acc_b[pl.ds(own, RB), cs] + up(sc.bf_recv[0, :, cs]) + up(sc.bf_recv[1, :, cs])

    chunks(last)

    for side in (0, 1):
        sent(sc.bh_recv.at[side], 2, side, 0)
        sent(sc.bf_send.at[side], 5, side, 0)

        def drain(i, c):
            sent(sc.h_recv.at[side, i], 0, side, i)
            sent(sc.f_send.at[side, i], 1, side, i)
            return c

        lax.fori_loop(0, 4, drain, 0)

    def drain_z(i, c):
        sent(sc.a_send.at[i], 3, 0, i)
        sent(sc.b_send.at[i], 4, 0, i)
        return c

    lax.fori_loop(1, 4, drain_z, 0)


class Refs:
    def __init__(self, **kw):
        self.__dict__.update(kw)


def scratch(width, hidden):
    bf, f32 = jnp.bfloat16, jnp.float32
    tokens = NX * NZ * (RA + RB)
    v = pltpu.VMEM
    return dict(
        xg=v((tokens, width), bf),
        og=v((tokens, width), bf),
        w_in=v((width, hidden), bf),
        w_out=v((width, hidden), bf),
        w_out_t=v((hidden, width), bf),
        act=v((tokens, hidden), bf),
        slope=v((tokens, hidden), f32),
        pre_grad=v((tokens, hidden), bf),
        tgt=v((RA + RB, width), bf),
        h_send=v((4, RA, width), bf),
        h_recv=v((2, 4, HA, width), bf),
        f_send=v((2, 4, RA, width), bf),
        f_recv=v((2, 4, RA, width), bf),
        a_send=v((4, RA, width), bf),
        a_recv=v((5, RA, width), bf),
        b_send=v((4, SUPER, width), bf),
        b_recv=v((5, SUPER, width), bf),
        bh_send=v((RB, width), bf),
        bh_recv=v((2, HB, width), bf),
        bf_send=v((2, RB, width), bf),
        bf_recv=v((2, RB, width), bf),
        acc_a=v((RA, width), f32),
        acc_b=v((SUPER, width), f32),
        fin_b=v((RB, width), f32),
        g1_send=pltpu.SemaphoreType.DMA((6, 2, 4)),
        g1_recv=pltpu.SemaphoreType.DMA((6, 2, 4)),
        g2_send=pltpu.SemaphoreType.DMA((6, 2, 4)),
        g2_recv=pltpu.SemaphoreType.DMA((6, 2, 4)),
        rs_send=pltpu.SemaphoreType.DMA((6, 2, 5)),
        rs_recv=pltpu.SemaphoreType.DMA((6, 2, 5)),
        local=pltpu.SemaphoreType.DMA((5,)),
    )


def step_kernel(names, width_scale, hidden_scale, tokens, x_ref, t_ref, keep_ref, w_ref, delta_ref, *refs):
    sc = Refs(**dict(zip(names, refs)))
    pp = Place()
    x, z, w = pp.x, pp.z, pp.w
    own_a, own_b = rows_a(x, z), rows_b(x, z)

    loads = [
        pltpu.make_async_copy(x_ref.at[pl.ds(0, RA)], sc.xg.at[pl.ds(own_a, RA)], sc.local.at[0]),
        pltpu.make_async_copy(x_ref.at[pl.ds(RA, RB)], sc.xg.at[pl.ds(own_b, RB)], sc.local.at[1]),
        pltpu.make_async_copy(w_ref.at[0], sc.w_in, sc.local.at[2]),
        pltpu.make_async_copy(w_ref.at[1], sc.w_out, sc.local.at[3]),
        pltpu.make_async_copy(t_ref, sc.tgt, sc.local.at[4]),
    ]
    for c in loads:
        c.start()

    barrier = pltpu.get_barrier_semaphore()
    for f in (pp.right, pp.left, pp.inner):
        pl.semaphore_signal(barrier, inc=1, device_id={"fsdp": f}, device_id_type=MESH)

    @pl.when(w == 1)
    def _():
        pl.semaphore_signal(barrier, inc=1, device_id={"fsdp": pp.edge}, device_id_type=MESH)

    pl.semaphore_wait(barrier, 3 + w)
    for c in loads:
        c.wait()

    def forward(start, n):
        rows = pl.ds(start, n)
        pre = jnp.dot(sc.xg[rows, :], sc.w_in[...], preferred_element_type=jnp.float32) * width_scale
        sig = jax.nn.sigmoid(pre)
        sc.act[rows, :] = (pre * sig).astype(jnp.bfloat16)
        sc.slope[rows, :] = sig * (1.0 + pre * (1.0 - sig))

    gather(pp, sc.xg, sc.g1_send, sc.g1_recv, forward)

    for k in range(0, sc.w_out.shape[0], 256):
        sc.w_out_t[:, k : k + 256] = sc.w_out[k : k + 256, :].T

    def partial(start, n, cs):
        return jnp.dot(sc.act[pl.ds(start, n), :], sc.w_out_t[:, cs], preferred_element_type=jnp.float32) * hidden_scale

    reduce(pp, partial, sc)

    def loss_grad(total, own, lo, n):
        res = sc.xg[pl.ds(own, n), :].astype(jnp.float32) + total[...] - sc.tgt[pl.ds(lo, n), :].astype(jnp.float32)
        sc.og[pl.ds(own, n), :] = (keep_ref[pl.ds(lo, n), :] * res / tokens).astype(jnp.bfloat16)

    loss_grad(sc.acc_a, own_a, 0, RA)
    loss_grad(sc.fin_b, own_b, RA, RB)

    def backward(start, n):
        rows = pl.ds(start, n)
        act_grad = jnp.dot(sc.og[rows, :], sc.w_out[...], preferred_element_type=jnp.float32) * hidden_scale
        sc.pre_grad[rows, :] = (act_grad * sc.slope[rows, :]).astype(jnp.bfloat16)

    gather(pp, sc.og, sc.g2_send, sc.g2_recv, backward)

    def grads(level, left, right, scale):
        def run(k, c):
            cols = pl.ds(pl.multiple_of(k * 256, 256), 256)
            g = lax.dot_general(
                left[:, cols], right[...], (((0,), (0,)), ((), ())), preferred_element_type=jnp.float32
            )
            delta_ref[level, cols, :] = (INNER_LR * scale * g).astype(jnp.bfloat16)
            return c

        lax.fori_loop(0, left.shape[1] // 256, run, 0)

    grads(1, sc.og, sc.act, hidden_scale)
    grads(0, sc.xg, sc.pre_grad, width_scale)


def per_device(inputs, targets, token_ids, module_table, path_weights, master, momentum):
    width, hidden = path_weights.shape[2:]
    n = lax.axis_size("fsdp")
    tokens = inputs.shape[1] * n
    keep = (token_ids[0] >= SPECIAL).astype(jnp.float32)[:, None]
    spec = scratch(width, hidden)
    hbm = pl.BlockSpec(memory_space=pl.ANY)
    vmem = pl.BlockSpec(memory_space=pltpu.VMEM)
    delta = pl.pallas_call(
        functools.partial(step_kernel, tuple(spec), width ** (-0.5), (hidden * n) ** (-0.5), tokens),
        out_shape=jax.ShapeDtypeStruct((2, width, hidden), jnp.bfloat16),
        in_specs=[hbm, hbm, vmem, hbm],
        out_specs=vmem,
        scratch_shapes=list(spec.values()),
        compiler_params=pltpu.CompilerParams(
            collective_id=0, has_side_effects=True, vmem_limit_bytes=62 * 1024 * 1024
        ),
        name="inner_step",
    )(inputs[0], targets[0], keep, path_weights[0])

    arrived = lax.all_to_all(delta[:, None], "path", split_axis=2, concat_axis=1, tiled=True).astype(jnp.float32)
    modules = master.shape[1]
    labels = jnp.arange(modules, dtype=jnp.int32)
    pick = (module_table.T[:, None, :] == labels[None, :, None]).astype(jnp.float32)
    counts = jnp.sum(pick, axis=2)
    sums = jnp.einsum("lmq,lqrc->lmrc", pick, arrived, precision=lax.Precision.HIGHEST)
    average = sums / counts[:, :, None, None]
    new_momentum = MOMENT * momentum + average
    new_master = master - OUTER_LR * (average + MOMENT * new_momentum)
    route = jnp.transpose(pick, (0, 2, 1)).astype(jnp.bfloat16)
    outgoing = jnp.einsum(
        "lqm,lmrc->lqrc", route, new_master.astype(jnp.bfloat16), preferred_element_type=jnp.float32
    ).astype(jnp.bfloat16)
    returned = lax.all_to_all(outgoing, "path", split_axis=1, concat_axis=2, tiled=True)
    new_weights = jnp.transpose(returned, (1, 0, 2, 3))
    return (new_weights, new_master, new_momentum)


def solution(mesh):
    in_specs = (
        P("path", "fsdp", None),
        P("path", "fsdp", None),
        P("path", "fsdp"),
        P(),
        P("path", None, None, "fsdp"),
        P(None, None, "path", "fsdp"),
        P(None, None, "path", "fsdp"),
    )
    out_specs = (
        P("path", None, None, "fsdp"),
        P(None, None, "path", "fsdp"),
        P(None, None, "path", "fsdp"),
    )
    return jax.shard_map(
        per_device, mesh=mesh, in_specs=in_specs, out_specs=out_specs, check_vma=False
    )
```

```python
import functools

import jax
import jax.numpy as jnp
from jax import lax
from jax.experimental import pallas as pl
from jax.experimental.pallas import tpu as pltpu
from jax.sharding import PartitionSpec as P

SPECIAL = 256
INNER_LR = 4096.0
OUTER_LR = 0.7
MOMENT = 0.9
MESH = pl.DeviceIdType.MESH

RA, RB = 96, 32
HA, HB = RA // 2, RB // 2
NX, NZ = 4, 4
ROWS_A = NX * NZ * RA
SUPER = NX * RB


class Place:
    def __init__(self):
        f = lax.axis_index("fsdp")
        self.x, self.z = f // NZ, f % NZ
        self.far = self.z // 2
        self.w = (self.z + self.far) % 2
        flip = 1 - 2 * self.far
        self.flip = flip
        self.right = ((self.x + 1) % NX) * NZ + self.z
        self.left = ((self.x + NX - 1) % NX) * NZ + self.z
        self.inner = self.x * NZ + self.z + flip
        self.edge = self.x * NZ + self.z - flip

    def zb(self, r):
        swap = jnp.where(r == 0, 1, jnp.where(r == 1, -1, 0))
        o = r + self.w * swap
        return o * self.flip + (NZ - 1) * self.far

    def col(self, dx):
        return (self.x + dx + NX) % NX


def rows_a(x, z):
    return pl.multiple_of((x * NZ + z) * RA, 16)


def rows_b(x, z):
    return pl.multiple_of(ROWS_A + (z * NX + x) * RB, 16)


def rows_super(z):
    return pl.multiple_of(ROWS_A + z * SUPER, 16)


def rcopy(src, dst, ssem, rsem, f):
    return pltpu.make_async_remote_copy(
        src_ref=src, dst_ref=dst, send_sem=ssem, recv_sem=rsem, device_id={"fsdp": f}, device_id_type=MESH
    )


def gather(pp, buf, ssem, rsem, compute):
    x, z, w = pp.x, pp.z, pp.w

    def piece(start, n):
        return buf.at[pl.ds(start, n)]

    def push(kind, side, i, start, n, f, slot):
        rcopy(piece(start, n), piece(start, n), ssem.at[kind, side, i], rsem.at[kind, slot[0], slot[1]], f).start()

    def arrived(kind, side, i, start, n):
        rcopy(piece(start, n), piece(start, n), ssem.at[kind, side, i], rsem.at[kind, side, i], pp.right).wait_recv()

    def sent(kind, side, i, n):
        rcopy(piece(0, n), piece(0, n), ssem.at[kind, side, i], rsem.at[kind, side, i], pp.right).wait_send()

    own_a, own_b = rows_a(x, z), rows_b(x, z)

    def z_own(kind, start, n):
        push(kind, 0, 0, start, n, pp.inner, (0, z))

        @pl.when(w == 1)
        def _():
            push(kind, 1, 0, start, n, pp.edge, (0, z))

    def z_forward(kind, r, zb, start, n):
        @pl.when((w == 1) & (r == 1))
        def _():
            push(kind, 0, r, start, n, pp.inner, (0, zb))

        @pl.when((w == 1) & (r >= 2))
        def _():
            push(kind, 1, r, start, n, pp.edge, (0, zb))

    z_own(0, own_a, RA)
    for side, f in ((0, pp.right), (1, pp.left)):
        push(3, side, 0, own_b, RB, f, (side, 0))

    def step(t, carry):
        zt = pp.zb(t)
        col_t = rows_a(x, zt)

        @pl.when((t >= 1) & (t <= 3))
        def _():
            arrived(0, 0, zt, col_t, RA)
            z_forward(0, t, zt, col_t, RA)

        @pl.when(t <= 3)
        def _():
            for side, f in ((0, pp.right), (1, pp.left)):
                push(1, side, t, col_t, RA, f, (side, t))

        @pl.when(t == 0)
        def _():
            for side, dx, f in ((0, -1, pp.right), (1, 1, pp.left)):
                start = rows_b(pp.col(dx), z)
                arrived(3, side, 0, start, RB)
                push(4, side, 0, pl.multiple_of(start + side * HB, 16), HB, f, (side, 0))

        zl = pp.zb(t - 1)

        @pl.when((t >= 1) & (t <= 4))
        def _():
            for side, dx, f in ((0, -1, pp.right), (1, 1, pp.left)):
                start = rows_a(pp.col(dx), zl)
                arrived(1, side, t - 1, start, RA)
                push(2, side, t - 1, pl.multiple_of(start + side * HA, 16), HA, f, (side, t - 1))

        @pl.when(t == 1)
        def _():
            start = rows_b(pp.col(2), z)
            for side in (0, 1):
                arrived(4, side, 0, pl.multiple_of(start + side * HB, 16), HB)
            z_own(5, rows_super(z), SUPER)

        @pl.when((t >= 2) & (t <= 4))
        def _():
            arrived(5, 0, zl, rows_super(zl), SUPER)
            z_forward(5, t - 1, zl, rows_super(zl), SUPER)

        @pl.when(t <= 3)
        def _():
            compute(col_t, RA)

        @pl.when((t >= 1) & (t <= 4))
        def _():
            def sides(j, c):
                compute(rows_a(pp.col(2 * j - 1), zl), RA)
                return c

            lax.fori_loop(0, 2, sides, 0)
            compute(rows_super(zl), SUPER)

        @pl.when(t >= 2)
        def _():
            start = rows_a(pp.col(2), pp.zb(t - 2))
            for side in (0, 1):
                arrived(2, side, t - 2, pl.multiple_of(start + side * HA, 16), HA)
            compute(start, RA)

        return carry

    lax.fori_loop(0, 6, step, 0)

    for kind, n in ((0, RA), (5, SUPER)):
        sent(kind, 0, 0, n)

        @pl.when(w == 1)
        def _():
            sent(kind, 1, 0, n)
            sent(kind, 0, 1, n)
            sent(kind, 1, 2, n)
            sent(kind, 1, 3, n)

    for side in (0, 1):
        sent(3, side, 0, RB)
        sent(4, side, 0, HB)

        def drain(i, c):
            sent(1, side, i, RA)
            sent(2, side, i, HA)
            return c

        lax.fori_loop(0, 4, drain, 0)


COLS = 512


def reduce(pp, partial, sc):
    x, z, w = pp.x, pp.z, pp.w
    width = sc.acc_a.shape[1]
    ssem, rsem = sc.rs_send, sc.rs_recv

    def chunks(body):
        def run(k, c):
            body(pl.ds(pl.multiple_of(k * COLS, 128), COLS))
            return c

        lax.fori_loop(0, width // COLS, run, 0)

    def push(src, dst, kind, side, i, f, slot):
        rcopy(src, dst, ssem.at[kind, side, i], rsem.at[kind, slot[0], slot[1]], f).start()

    def arrived(ref, kind, side, i):
        rcopy(ref, ref, ssem.at[kind, side, i], rsem.at[kind, side, i], pp.right).wait_recv()

    def sent(ref, kind, side, i):
        rcopy(ref, ref, ssem.at[kind, side, i], rsem.at[kind, side, i], pp.right).wait_send()

    def up(v):
        return v.astype(jnp.float32)

    def z_stage(kind, r, acc, recv, send):
        @pl.when((w == 1) & (r >= 1))
        def _():
            arrived(recv.at[r], kind, 0, r)

            def add(cs):
                send[r - 1, :, cs] = (acc[:, cs] + up(recv[r, :, cs])).astype(jnp.bfloat16)

            chunks(add)

        @pl.when((w == 1) & (r >= 2))
        def _():
            slot = jnp.where(r == 3, 1, 0)
            push(send.at[r - 1], recv.at[slot], kind, 0, r, pp.inner, (0, slot))

        @pl.when((w == 1) & (r == 1))
        def _():
            push(send.at[r - 1], recv.at[0], kind, 0, r, pp.edge, (0, 0))

        @pl.when((w == 0) & (r >= 1))
        def _():
            def cast(cs):
                send[r - 1, :, cs] = acc[:, cs].astype(jnp.bfloat16)

            chunks(cast)
            slot = jnp.where(r == 1, 4, r)
            push(send.at[r - 1], recv.at[slot], kind, 0, r, pp.inner, (0, slot))

        @pl.when(r == 0)
        def _():
            arrived(recv.at[0], kind, 0, 0)

            def add(cs):
                acc[:, cs] = acc[:, cs] + up(recv[0, :, cs])

            chunks(add)

        @pl.when((w == 1) & (r == 0))
        def _():
            arrived(recv.at[4], kind, 0, 4)

            def add(cs):
                acc[:, cs] = acc[:, cs] + up(recv[4, :, cs])

            chunks(add)

    def b_round(r):
        start = rows_super(pp.zb(r))

        def fill(cs):
            sc.acc_b[:, cs] = partial(start, SUPER, cs)

        chunks(fill)
        z_stage(4, r, sc.acc_b, sc.b_recv, sc.b_send)

    def step(t, carry):
        r0, r1, r2 = 3 - t, 4 - t, 5 - t

        @pl.when(t <= 3)
        def _():
            start = rows_a(pp.col(2), pp.zb(r0))

            def fill(cs):
                sc.h_send[r0, :, cs] = partial(start, RA, cs).astype(jnp.bfloat16)

            chunks(fill)
            push(sc.h_send.at[r0, pl.ds(0, HA)], sc.h_recv.at[1, r0], 0, 1, r0, pp.left, (1, r0))
            push(sc.h_send.at[r0, pl.ds(HA, HA)], sc.h_recv.at[0, r0], 0, 0, r0, pp.right, (0, r0))

        @pl.when((t == 0) & (w == 0))
        def _():
            def run(i, c):
                b_round(3 - i)
                return c

            lax.fori_loop(0, 3, run, 0)

        @pl.when((t >= 1) & (t <= 4))
        def _():
            zr = pp.zb(r1)
            for side, dx, f, lo in ((0, 1, pp.right, HA), (1, -1, pp.left, 0)):
                start = rows_a(pp.col(dx), zr)
                arrived(sc.h_recv.at[side, r1], 0, side, r1)

                def fill(cs):
                    part = partial(start, RA, cs)
                    got = up(sc.h_recv[side, r1, :, cs])
                    both = part[lo : lo + HA] + got
                    alone = part[HA - lo : HA - lo + HA]
                    sc.f_send[side, r1, pl.ds(lo, HA), cs] = both.astype(jnp.bfloat16)
                    sc.f_send[side, r1, pl.ds(HA - lo, HA), cs] = alone.astype(jnp.bfloat16)

                chunks(fill)
                push(sc.f_send.at[side, r1], sc.f_recv.at[side, r1], 1, side, r1, f, (side, r1))

        @pl.when((t >= 1) & (t <= 3) & (w == 1))
        def _():
            b_round(r1)

        @pl.when(t == 4)
        def _():
            b_round(0)
            start = pl.multiple_of(pp.col(2) * RB, RB)
            sc.bh_send[...] = sc.acc_b[pl.ds(start, RB), :].astype(jnp.bfloat16)
            push(sc.bh_send.at[pl.ds(0, HB)], sc.bh_recv.at[1], 2, 1, 0, pp.left, (1, 0))
            push(sc.bh_send.at[pl.ds(HB, HB)], sc.bh_recv.at[0], 2, 0, 0, pp.right, (0, 0))

        @pl.when(t >= 2)
        def _():
            start = rows_a(x, pp.zb(r2))
            for side in (0, 1):
                arrived(sc.f_recv.at[side, r2], 1, side, r2)

            def fill(cs):
                sc.acc_a[:, cs] = partial(start, RA, cs) + up(sc.f_recv[0, r2, :, cs]) + up(sc.f_recv[1, r2, :, cs])

            chunks(fill)
            z_stage(3, r2, sc.acc_a, sc.a_recv, sc.a_send)

        @pl.when(t == 4)
        def _():
            for side, dx, f, lo in ((0, 1, pp.right, HB), (1, -1, pp.left, 0)):
                start = pl.multiple_of(pp.col(dx) * RB, RB)
                arrived(sc.bh_recv.at[side], 2, side, 0)

                def fill(cs):
                    got = up(sc.bh_recv[side, :, cs])
                    both = sc.acc_b[pl.ds(pl.multiple_of(start + lo, 8), HB), cs] + got
                    alone = sc.acc_b[pl.ds(pl.multiple_of(start + HB - lo, 8), HB), cs]
                    sc.bf_send[side, pl.ds(lo, HB), cs] = both.astype(jnp.bfloat16)
                    sc.bf_send[side, pl.ds(HB - lo, HB), cs] = alone.astype(jnp.bfloat16)

                chunks(fill)
                push(sc.bf_send.at[side], sc.bf_recv.at[side], 5, side, 0, f, (side, 0))

        return carry

    lax.fori_loop(0, 6, step, 0)
    for side in (0, 1):
        arrived(sc.bf_recv.at[side], 5, side, 0)
    own = pl.multiple_of(x * RB, RB)

    def last(cs):
        sc.fin_b[:, cs] = sc.acc_b[pl.ds(own, RB), cs] + up(sc.bf_recv[0, :, cs]) + up(sc.bf_recv[1, :, cs])

    chunks(last)

    for side in (0, 1):
        sent(sc.bh_recv.at[side], 2, side, 0)
        sent(sc.bf_send.at[side], 5, side, 0)

        def drain(i, c):
            sent(sc.h_recv.at[side, i], 0, side, i)
            sent(sc.f_send.at[side, i], 1, side, i)
            return c

        lax.fori_loop(0, 4, drain, 0)

    def drain_z(i, c):
        sent(sc.a_send.at[i - 1], 3, 0, i)
        sent(sc.b_send.at[i - 1], 4, 0, i)
        return c

    lax.fori_loop(1, 4, drain_z, 0)


class Refs:
    def __init__(self, **kw):
        self.__dict__.update(kw)


def scratch(width, hidden, modules, rows):
    bf, f32 = jnp.bfloat16, jnp.float32
    tokens = NX * NZ * (RA + RB)
    v = pltpu.VMEM
    return dict(
        xg=v((tokens, width), bf),
        og=v((tokens, width), bf),
        w_in=v((hidden, width), bf),
        w_out=v((hidden, width), bf),
        act=v((tokens, hidden), bf),
        slope=v((tokens, hidden), f32),
        pre_grad=v((tokens, hidden), bf),
        tgt=v((RA + RB, width), bf),
        h_send=v((4, RA, width), bf),
        h_recv=v((2, 4, HA, width), bf),
        f_send=v((2, 4, RA, width), bf),
        f_recv=v((2, 4, RA, width), bf),
        a_send=v((3, RA, width), bf),
        a_recv=v((5, RA, width), bf),
        b_send=v((3, SUPER, width), bf),
        b_recv=v((5, SUPER, width), bf),
        bh_send=v((RB, width), bf),
        bh_recv=v((2, HB, width), bf),
        bf_send=v((2, RB, width), bf),
        bf_recv=v((2, RB, width), bf),
        acc_a=v((RA, width), f32),
        acc_b=v((SUPER, width), f32),
        fin_b=v((RB, width), f32),
        g1_send=pltpu.SemaphoreType.DMA((6, 2, 4)),
        g1_recv=pltpu.SemaphoreType.DMA((6, 2, 4)),
        g2_send=pltpu.SemaphoreType.DMA((6, 2, 4)),
        g2_recv=pltpu.SemaphoreType.DMA((6, 2, 4)),
        rs_send=pltpu.SemaphoreType.DMA((6, 2, 5)),
        rs_recv=pltpu.SemaphoreType.DMA((6, 2, 5)),
        local=pltpu.SemaphoreType.DMA((7,)),
        d_send=v((2, 2, HALF, hidden, rows), bf),
        d_recv=v((2, 2, HALF, hidden, rows), bf),
        z_send=v((2, modules, hidden, rows), bf),
        z_recv=v((2, modules, hidden, rows), bf),
        fresh=v((2, modules, hidden, rows), bf),
        far_0=v((modules, hidden, rows), bf),
        far_1=v((modules, hidden, rows), bf),
        mast=v((2, modules, hidden, rows), f32),
        mom=v((2, modules, hidden, rows), f32),
        ds=pltpu.SemaphoreType.DMA((2, 2, HALF)),
        dr=pltpu.SemaphoreType.DMA((2, 2, HALF)),
        os=pltpu.SemaphoreType.DMA((2, 2, HALF)),
        orv=pltpu.SemaphoreType.DMA((2, 2, HALF)),
        zs=pltpu.SemaphoreType.DMA((2, 2)),
        zr=pltpu.SemaphoreType.DMA((2, 2)),
        out=pltpu.SemaphoreType.DMA((2, 2)),
    )


HALF = 8
PATHS_PER_MODULE = 4


class Group:
    def __init__(self):
        p = lax.axis_index("path")
        self.h, self.i = p // HALF, p % HALF
        self.y, self.c = self.i // 2, self.i % 2
        self.across = (1 - self.h) * HALF + self.i

    def peer(self, i):
        return self.h * HALF + i


def pcopy(src, dst, ssem, rsem, p):
    return pltpu.make_async_remote_copy(
        src_ref=src, dst_ref=dst, send_sem=ssem, recv_sem=rsem, device_id={"path": p}, device_id_type=MESH
    )


def path_phase(pg, sc, width_scale, hidden_scale, table, new_w, new_mast, new_mom):
    h, me = pg.h, pg.i
    hidden, rows = sc.mast.shape[2:]
    modules = sc.mast.shape[1]
    operands = ((sc.xg, sc.pre_grad, width_scale), (sc.og, sc.act, hidden_scale))

    def half(side):
        return h if side == 0 else 1 - h

    def dcopy(level, side, i, src):
        return pcopy(sc.d_send.at[level, side, i], sc.d_recv.at[level, side, src], sc.ds.at[level, side, i], sc.dr.at[level, side, src], pg.peer(i))

    def changes(level, side):
        left, right, scale = operands[level]

        def run(k, c):
            d = jnp.where(k == 0, 2, jnp.where(k == 1, 1, jnp.where(k == 2, 3, 0)))
            y = (pg.y + d) % 4
            cols = pl.ds(pl.multiple_of((half(side) * HALF + 2 * y) * rows, 128), 2 * rows)
            g = lax.dot_general(right[...], left[:, cols], (((0,), (0,)), ((), ())), preferred_element_type=jnp.float32)
            g = (INNER_LR * scale * g).astype(jnp.bfloat16)
            for core in (0, 1):
                i = 2 * y + core
                part = g[:, core * rows : (core + 1) * rows]

                @pl.when(i == me)
                def _():
                    sc.d_recv[level, side, i] = part

                @pl.when(i != me)
                def _():
                    sc.d_send[level, side, i] = part
                    dcopy(level, side, i, me).start()

            return c

        lax.fori_loop(0, 4, run, 0)

    def await_changes(level, side):
        def run(i, c):
            @pl.when(i != me)
            def _():
                dcopy(level, side, i, i).wait_recv()

            return c

        lax.fori_loop(0, HALF, run, 0)

    STEP = 32

    def sums(level, side, use):
        def run(k, c):
            part = pl.ds(pl.multiple_of(k * STEP, STEP), STEP)
            total = [jnp.zeros((STEP, rows), jnp.float32) for _ in range(modules)]
            for i in range(HALF):
                change = sc.d_recv[level, side, i, part, :].astype(jnp.float32)
                named = table[pg.peer(i), level]
                for m in range(modules):
                    total[m] = total[m] + jnp.where(named == m, 1.0, 0.0) * change
            for m in range(modules):
                use(m, part, total[m])
            return c

        lax.fori_loop(0, hidden // STEP, run, 0)

    far = (sc.far_0, sc.far_1)

    def zcopy(kind, level):
        src, dst = (sc.z_send.at[level], sc.z_recv.at[level]) if kind == 0 else (sc.fresh.at[level], far[level])
        return pcopy(src, dst, sc.zs.at[kind, level], sc.zr.at[kind, level], pg.across)

    def sums_across(level):
        await_changes(level, 1)

        def use(m, part, total):
            sc.z_send[level, m, part, :] = total.astype(jnp.bfloat16)

        sums(level, 1, use)
        zcopy(0, level).start()

    def outs(level):
        return [
            pltpu.make_async_copy(sc.mast.at[level], new_mast.at[level], sc.out.at[0, level]),
            pltpu.make_async_copy(sc.mom.at[level], new_mom.at[level], sc.out.at[1, level]),
        ]

    def update(level):
        await_changes(level, 0)
        zcopy(0, level).wait_recv()

        def use(m, part, total):
            average = (total + sc.z_recv[level, m, part, :].astype(jnp.float32)) * (1.0 / PATHS_PER_MODULE)
            moved = MOMENT * sc.mom[level, m, part, :] + average
            master = sc.mast[level, m, part, :] - OUTER_LR * (average + MOMENT * moved)
            sc.mom[level, m, part, :] = moved
            sc.mast[level, m, part, :] = master
            sc.fresh[level, m, part, :] = master.astype(jnp.bfloat16)

        sums(level, 0, use)
        zcopy(1, level).start()
        for c in outs(level):
            c.start()

    def ocopy(level, side, i, src):
        place = pl.ds(pl.multiple_of((half(side) * HALF + src) * rows, 128), rows)
        return pcopy(sc.d_send.at[level, side, i], new_w.at[level, :, place], sc.os.at[level, side, i], sc.orv.at[level, side, src], pg.peer(i))

    def own_copy(level, side):
        place = pl.ds(pl.multiple_of((half(side) * HALF + me) * rows, 128), rows)
        return pltpu.make_async_copy(sc.d_send.at[level, side, me], new_w.at[level, :, place], sc.os.at[level, side, me])

    def hand_back(level, side):
        if side == 1:
            zcopy(1, level).wait_recv()

        def run(k, c):
            i = (me + 1 + k) % HALF

            @pl.when(i != me)
            def _():
                dcopy(level, side, i, me).wait_send()

            named = table[pg.peer(i), level]
            sc.d_send[level, side, i] = sc.fresh[level, named] if side == 0 else far[level][named]

            @pl.when(i != me)
            def _():
                ocopy(level, side, i, me).start()

            @pl.when(i == me)
            def _():
                own_copy(level, side).start()

            return c

        lax.fori_loop(0, HALF, run, 0)

    changes(1, 1)
    changes(0, 1)
    changes(1, 0)
    sums_across(1)
    changes(0, 0)
    sums_across(0)
    update(1)
    hand_back(1, 0)
    update(0)
    hand_back(0, 0)
    hand_back(1, 1)
    hand_back(0, 1)

    for level in (0, 1):
        for side in (0, 1):
            own_copy(level, side).wait()

            def drain(i, c):
                @pl.when(i != me)
                def _():
                    ocopy(level, side, i, i).wait_recv()
                    ocopy(level, side, i, me).wait_send()

                return c

            lax.fori_loop(0, HALF, drain, 0)
        zcopy(0, level).wait_send()
        zcopy(1, level).wait_send()
        for c in outs(level):
            c.wait()


def step_kernel(names, width_scale, hidden_scale, tokens, x_ref, t_ref, keep_ref, table_ref, w_ref, mast_ref, mom_ref,
                new_w_ref, new_mast_ref, new_mom_ref, *refs):
    sc = Refs(**dict(zip(names, refs)))
    pp = Place()
    pg = Group()
    x, z, w = pp.x, pp.z, pp.w
    own_a, own_b = rows_a(x, z), rows_b(x, z)

    loads = [
        pltpu.make_async_copy(x_ref.at[pl.ds(0, RA)], sc.xg.at[pl.ds(own_a, RA)], sc.local.at[0]),
        pltpu.make_async_copy(x_ref.at[pl.ds(RA, RB)], sc.xg.at[pl.ds(own_b, RB)], sc.local.at[1]),
        pltpu.make_async_copy(w_ref.at[0], sc.w_in, sc.local.at[2]),
        pltpu.make_async_copy(w_ref.at[1], sc.w_out, sc.local.at[3]),
        pltpu.make_async_copy(t_ref, sc.tgt, sc.local.at[4]),
        pltpu.make_async_copy(mast_ref, sc.mast, sc.local.at[5]),
        pltpu.make_async_copy(mom_ref, sc.mom, sc.local.at[6]),
    ]
    for c in loads:
        c.start()

    barrier = pltpu.get_barrier_semaphore()
    for f in (pp.right, pp.left, pp.inner):
        pl.semaphore_signal(barrier, inc=1, device_id={"fsdp": f}, device_id_type=MESH)

    @pl.when(w == 1)
    def _():
        pl.semaphore_signal(barrier, inc=1, device_id={"fsdp": pp.edge}, device_id_type=MESH)

    for i in range(HALF):

        @pl.when(pg.i != i)
        def _():
            pl.semaphore_signal(barrier, inc=1, device_id={"path": pg.peer(i)}, device_id_type=MESH)

    pl.semaphore_signal(barrier, inc=1, device_id={"path": pg.across}, device_id_type=MESH)
    pl.semaphore_wait(barrier, 3 + HALF + w)
    for c in loads:
        c.wait()

    def across_width(rows, weights):
        return lax.dot_general(rows, weights[...], (((1,), (1,)), ((), ())), preferred_element_type=jnp.float32)

    def forward(start, n):
        rows = pl.ds(start, n)
        pre = across_width(sc.xg[rows, :], sc.w_in) * width_scale
        sig = jax.nn.sigmoid(pre)
        sc.act[rows, :] = (pre * sig).astype(jnp.bfloat16)
        sc.slope[rows, :] = sig * (1.0 + pre * (1.0 - sig))

    gather(pp, sc.xg, sc.g1_send, sc.g1_recv, forward)

    def partial(start, n, cs):
        return jnp.dot(sc.act[pl.ds(start, n), :], sc.w_out[:, cs], preferred_element_type=jnp.float32) * hidden_scale

    reduce(pp, partial, sc)

    def loss_grad(total, own, lo, n):
        res = sc.xg[pl.ds(own, n), :].astype(jnp.float32) + total[...] - sc.tgt[pl.ds(lo, n), :].astype(jnp.float32)
        sc.og[pl.ds(own, n), :] = (keep_ref[pl.ds(lo, n), :] * res / tokens).astype(jnp.bfloat16)

    loss_grad(sc.acc_a, own_a, 0, RA)
    loss_grad(sc.fin_b, own_b, RA, RB)

    def backward(start, n):
        rows = pl.ds(start, n)
        act_grad = across_width(sc.og[rows, :], sc.w_out) * hidden_scale
        sc.pre_grad[rows, :] = (act_grad * sc.slope[rows, :]).astype(jnp.bfloat16)

    gather(pp, sc.og, sc.g2_send, sc.g2_recv, backward)

    path_phase(pg, sc, width_scale, hidden_scale, table_ref, new_w_ref, new_mast_ref, new_mom_ref)


def turn(v):
    return jnp.swapaxes(v, -1, -2)


def per_device(inputs, targets, token_ids, module_table, path_weights, master, momentum):
    width, hidden = path_weights.shape[2:]
    n = lax.axis_size("fsdp")
    tokens = inputs.shape[1] * n
    keep = (token_ids[0] >= SPECIAL).astype(jnp.float32)[:, None]
    modules, rows = master.shape[1:3]
    spec = scratch(width, hidden, modules, rows)
    hbm = pl.BlockSpec(memory_space=pl.ANY)
    vmem = pl.BlockSpec(memory_space=pltpu.VMEM)
    smem = pl.BlockSpec(memory_space=pltpu.SMEM)
    new_weights, new_master, new_momentum = pl.pallas_call(
        functools.partial(step_kernel, tuple(spec), width ** (-0.5), (hidden * n) ** (-0.5), tokens),
        out_shape=(
            jax.ShapeDtypeStruct((2, hidden, width), jnp.bfloat16),
            jax.ShapeDtypeStruct((2, modules, hidden, rows), jnp.float32),
            jax.ShapeDtypeStruct((2, modules, hidden, rows), jnp.float32),
        ),
        in_specs=[hbm, hbm, vmem, smem, hbm, hbm, hbm],
        out_specs=(hbm, hbm, hbm),
        scratch_shapes=list(spec.values()),
        compiler_params=pltpu.CompilerParams(
            collective_id=0, has_side_effects=True, vmem_limit_bytes=63 * 1024 * 1024
        ),
        name="outer_step",
    )(inputs[0], targets[0], keep, module_table, turn(path_weights[0]), turn(master), turn(momentum))
    return (turn(new_weights)[None], turn(new_master), turn(new_momentum))


def solution(mesh):
    in_specs = (
        P("path", "fsdp", None),
        P("path", "fsdp", None),
        P("path", "fsdp"),
        P(),
        P("path", None, None, "fsdp"),
        P(None, None, "path", "fsdp"),
        P(None, None, "path", "fsdp"),
    )
    out_specs = (
        P("path", None, None, "fsdp"),
        P(None, None, "path", "fsdp"),
        P(None, None, "path", "fsdp"),
    )
    return jax.shard_map(
        per_device, mesh=mesh, in_specs=in_specs, out_specs=out_specs, check_vma=False
    )
```

```python
import functools

import jax
import jax.numpy as jnp
from jax import lax
from jax.experimental import pallas as pl
from jax.experimental.pallas import tpu as pltpu
from jax.sharding import PartitionSpec as P

SPECIAL = 256
INNER_LR = 4096.0
OUTER_LR = 0.7
MOMENT = 0.9
MESH = pl.DeviceIdType.MESH

CHUNKS = 2
RA, RB = 48, 16
NX, NZ = 4, 4
LINE = NX * RA
SUPER = NX * RB
ROWS_A = NZ * LINE
CHUNK = ROWS_A + NZ * SUPER
OWN = RA + RB


class Place:
    def __init__(self):
        f = lax.axis_index("fsdp")
        self.x, self.z = f // NZ, f % NZ
        self.far = self.z // 2
        self.w = (self.z + self.far) % 2
        flip = 1 - 2 * self.far
        self.flip = flip
        self.right = ((self.x + 1) % NX) * NZ + self.z
        self.left = ((self.x + NX - 1) % NX) * NZ + self.z
        self.inner = self.x * NZ + self.z + flip
        self.edge = self.x * NZ + self.z - flip

    def zb(self, r):
        swap = jnp.where(r == 0, 1, jnp.where(r == 1, -1, 0))
        o = r + self.w * swap
        return o * self.flip + (NZ - 1) * self.far

    def col(self, dx):
        return (self.x + dx + NX) % NX


def rows_line(c, z):
    return pl.multiple_of(c * CHUNK + z * LINE, 16)


def rows_a(c, x, z):
    return pl.multiple_of(c * CHUNK + z * LINE + x * RA, 16)


def rows_b(c, x, z):
    return pl.multiple_of(c * CHUNK + ROWS_A + z * SUPER + x * RB, 16)


def rows_super(c, z):
    return pl.multiple_of(c * CHUNK + ROWS_A + z * SUPER, 16)


def rcopy(src, dst, ssem, rsem, f):
    return pltpu.make_async_remote_copy(
        src_ref=src, dst_ref=dst, send_sem=ssem, recv_sem=rsem, device_id={"fsdp": f}, device_id_type=MESH
    )


STEPS = 6


class Gather:
    FIRST = (0, 4, 12, 20, 22, 24)
    PER_SIDE = (4, 4, 4, 1, 1, 4)
    RECV = 28

    def __init__(self, pp, chunk, buf, ssem, rsem, compute):
        self.pp, self.chunk, self.buf, self.ssem, self.rsem, self.compute = pp, chunk, buf, ssem, rsem, compute
        self.half = buf.shape[1] // 2

    def piece(self, start, n, side=None):
        if side is None:
            return self.buf.at[pl.ds(start, n)]
        return self.buf.at[pl.ds(start, n), pl.ds(side * self.half, self.half)]

    def copy(self, kind, side, i, ref, f, slot):
        c = self.chunk
        got = self.FIRST[kind] + slot[0] * self.PER_SIDE[kind] + slot[1]
        return rcopy(ref, ref, self.ssem.at[c, kind], self.rsem.at[c, got], f)

    def push(self, kind, side, i, ref, f, slot):
        self.copy(kind, side, i, ref, f, slot).start()

    def arrived(self, kind, side, i, ref):
        self.copy(kind, side, i, ref, self.pp.right, (side, i)).wait_recv()

    def sent(self, kind, n):
        self.copy(kind, 0, 0, self.piece(0, n), self.pp.right, (0, 0)).wait_send()

    def z_own(self, kind, ref):
        pp = self.pp
        self.push(kind, 0, 0, ref, pp.inner, (0, pp.z))

        @pl.when(pp.w == 1)
        def _():
            self.push(kind, 1, 0, ref, pp.edge, (0, pp.z))

    def z_forward(self, kind, r, zb, ref):
        pp = self.pp

        @pl.when((pp.w == 1) & (r == 1))
        def _():
            self.push(kind, 0, r, ref, pp.inner, (0, zb))

        @pl.when((pp.w == 1) & (r >= 2))
        def _():
            self.push(kind, 1, r, ref, pp.edge, (0, zb))

    def start(self):
        pp, c = self.pp, self.chunk
        self.z_own(0, self.piece(rows_a(c, pp.x, pp.z), RA))
        for side, f in ((0, pp.right), (1, pp.left)):
            self.push(3, side, 0, self.piece(rows_b(c, pp.x, pp.z), RB), f, (side, 0))

    def step(self, t):
        pp, c = self.pp, self.chunk
        z = pp.z
        sides = ((0, -1, pp.right), (1, 1, pp.left))
        zt, zl = pp.zb(t), pp.zb(t - 1)

        @pl.when((t >= 1) & (t <= 3))
        def _():
            ref = self.piece(rows_a(c, pp.x, zt), RA)
            self.arrived(0, 0, zt, ref)
            self.z_forward(0, t, zt, ref)

        @pl.when(t <= 3)
        def _():
            for side, _, f in sides:
                self.push(1, side, t, self.piece(rows_a(c, pp.x, zt), RA), f, (side, t))

        @pl.when(t == 0)
        def _():
            for side, dx, f in sides:
                start = rows_b(c, pp.col(dx), z)
                self.arrived(3, side, 0, self.piece(start, RB))
                self.push(4, side, 0, self.piece(start, RB, side), f, (side, 0))

        @pl.when((t >= 1) & (t <= 4))
        def _():
            for side, dx, f in sides:
                start = rows_a(c, pp.col(dx), zl)
                self.arrived(1, side, t - 1, self.piece(start, RA))
                self.push(2, side, t - 1, self.piece(start, RA, side), f, (side, t - 1))

        @pl.when(t == 1)
        def _():
            for side in (0, 1):
                self.arrived(4, side, 0, self.piece(rows_b(c, pp.col(2), z), RB, side))
            self.z_own(5, self.piece(rows_super(c, z), SUPER))

        @pl.when((t >= 2) & (t <= 4))
        def _():
            ref = self.piece(rows_super(c, zl), SUPER)
            self.arrived(5, 0, zl, ref)
            self.z_forward(5, t - 1, zl, ref)

        @pl.when((t >= 1) & (t <= 4))
        def _():
            self.compute(rows_super(c, zl), SUPER)

        @pl.when(t >= 2)
        def _():
            zo = pp.zb(t - 2)
            for side in (0, 1):
                self.arrived(2, side, t - 2, self.piece(rows_a(c, pp.col(2), zo), RA, side))
            self.compute(rows_line(c, zo), LINE)

    def finish(self):
        for kind, n in ((0, RA), (5, SUPER)):

            @pl.when(self.pp.w == 0)
            def _():
                self.sent(kind, n)

            @pl.when(self.pp.w == 1)
            def _():
                self.sent(kind, 5 * n)

        for kind, n in ((1, 8 * RA), (2, 4 * RA), (3, 2 * RB), (4, RB)):
            self.sent(kind, n)


COLS = 512


def up(v):
    return v.astype(jnp.float32)


class Reduce:
    def __init__(self, pp, chunk, partial, sc):
        self.pp, self.chunk, self.partial, self.sc = pp, chunk, partial, sc
        self.width = sc.acc_a.shape[-1]

    def over(self, body, first=0, width=None):
        def run(k, carry):
            body(pl.ds(pl.multiple_of(first + k * COLS, 128), COLS))
            return carry

        lax.fori_loop(0, (width or self.width) // COLS, run, 0)

    FIRST = (0, 8, 16, 18, 23, 28)
    PER_SIDE = (4, 4, 1, 5, 5, 1)
    RECV = 30

    def copy(self, src, dst, kind, side, i, f, slot):
        c, sc = self.chunk, self.sc
        got = self.FIRST[kind] + slot[0] * self.PER_SIDE[kind] + slot[1]
        return rcopy(src, dst, sc.rs_send.at[c, kind], sc.rs_recv.at[c, got], f)

    def push(self, src, dst, kind, side, i, f, slot):
        self.copy(src, dst, kind, side, i, f, slot).start()

    def arrived(self, ref, kind, side, i):
        self.copy(ref, ref, kind, side, i, self.pp.right, (side, i)).wait_recv()

    def sent(self, ref, kind):
        self.copy(ref, ref, kind, 0, 0, self.pp.right, (0, 0)).wait_send()

    def z_stage(self, kind, r, acc, recv, send):
        pp, c, w = self.pp, self.chunk, self.pp.w

        @pl.when((w == 1) & (r >= 1))
        def _():
            self.arrived(recv.at[c, r], kind, 0, r)

            def add(cs):
                send[c, r - 1, :, cs] = (acc[c, :, cs] + up(recv[c, r, :, cs])).astype(jnp.bfloat16)

            self.over(add)

        @pl.when((w == 1) & (r >= 2))
        def _():
            slot = jnp.where(r == 3, 1, 0)
            self.push(send.at[c, r - 1], recv.at[c, slot], kind, 0, r, pp.inner, (0, slot))

        @pl.when((w == 1) & (r == 1))
        def _():
            self.push(send.at[c, r - 1], recv.at[c, 0], kind, 0, r, pp.edge, (0, 0))

        @pl.when((w == 0) & (r >= 1))
        def _():
            def cast(cs):
                send[c, r - 1, :, cs] = acc[c, :, cs].astype(jnp.bfloat16)

            self.over(cast)
            slot = jnp.where(r == 1, 4, r)
            self.push(send.at[c, r - 1], recv.at[c, slot], kind, 0, r, pp.inner, (0, slot))

        def last(i):
            self.arrived(recv.at[c, i], kind, 0, i)

            def add(cs):
                acc[c, :, cs] = acc[c, :, cs] + up(recv[c, i, :, cs])

            self.over(add)

        @pl.when(r == 0)
        def _():
            last(0)

        @pl.when((w == 1) & (r == 0))
        def _():
            last(4)

    def b_round(self, r):
        sc, c = self.sc, self.chunk
        start = rows_super(c, self.pp.zb(r))

        def fill(cs):
            sc.acc_b[c, :, cs] = self.partial(start, SUPER, cs)

        self.over(fill)
        self.z_stage(4, r, sc.acc_b, sc.b_recv, sc.b_send)

    def step(self, t):
        pp, sc, c, w = self.pp, self.sc, self.chunk, self.pp.w
        r0, r1, r2 = 3 - t, 4 - t, 5 - t
        half = self.width // 2

        def rows(dx, n):
            return pl.ds(pl.multiple_of(pp.col(dx) * n, 16), n)

        sides = ((0, 1, pp.right, half), (1, -1, pp.left, 0))

        @pl.when(t <= 3)
        def _():
            start = rows_line(c, pp.zb(r0))

            def fill(cs):
                sc.part[c, r0, :, cs] = self.partial(start, LINE, cs).astype(jnp.bfloat16)

            self.over(fill)
            for side, _, f, lo in sides:
                src = sc.part.at[c, r0, rows(2, RA), pl.ds(lo, half)]
                self.push(src, sc.h_recv.at[c, side, r0], 0, side, r0, f, (side, r0))

        @pl.when((t == 0) & (w == 0))
        def _():
            def run(i, carry):
                self.b_round(3 - i)
                return carry

            lax.fori_loop(0, 3, run, 0)

        @pl.when((t >= 1) & (t <= 4))
        def _():
            for side, dx, f, lo in sides:
                self.arrived(sc.h_recv.at[c, side, r1], 0, side, r1)
                where = rows(dx, RA)

                def add(cs):
                    to = pl.ds(pl.multiple_of(lo + cs.start, 128), COLS)
                    sc.part[c, r1, where, to] = (up(sc.part[c, r1, where, to]) + up(sc.h_recv[c, side, r1, :, cs])).astype(jnp.bfloat16)

                self.over(add, width=half)
                self.push(sc.part.at[c, r1, where], sc.f_recv.at[c, side, r1], 1, side, r1, f, (side, r1))

        @pl.when((t >= 1) & (t <= 3) & (w == 1))
        def _():
            self.b_round(r1)

        @pl.when(t == 4)
        def _():
            self.b_round(0)
            sc.bh_send[c] = sc.acc_b[c, rows(2, RB), :].astype(jnp.bfloat16)
            for side, _, f, lo in sides:
                self.push(sc.bh_send.at[c, :, pl.ds(lo, half)], sc.bh_recv.at[c, side], 2, side, 0, f, (side, 0))

        @pl.when(t >= 2)
        def _():
            for side in (0, 1):
                self.arrived(sc.f_recv.at[c, side, r2], 1, side, r2)
            where = rows(0, RA)

            def fill(cs):
                sc.acc_a[c, :, cs] = up(sc.part[c, r2, where, cs]) + up(sc.f_recv[c, 0, r2, :, cs]) + up(sc.f_recv[c, 1, r2, :, cs])

            self.over(fill)
            self.z_stage(3, r2, sc.acc_a, sc.a_recv, sc.a_send)

        @pl.when(t == 4)
        def _():
            for side, dx, f, lo in sides:
                self.arrived(sc.bh_recv.at[c, side], 2, side, 0)
                where = rows(dx, RB)
                got, alone = pl.ds(lo, half), pl.ds(half - lo, half)
                sc.bf_send[c, side, :, got] = (sc.acc_b[c, where, got] + up(sc.bh_recv[c, side])).astype(jnp.bfloat16)
                sc.bf_send[c, side, :, alone] = sc.acc_b[c, where, alone].astype(jnp.bfloat16)
                self.push(sc.bf_send.at[c, side], sc.bf_recv.at[c, side], 5, side, 0, f, (side, 0))

    def finish(self):
        pp, sc, c = self.pp, self.sc, self.chunk
        for side in (0, 1):
            self.arrived(sc.bf_recv.at[c, side], 5, side, 0)
        own = pl.multiple_of(pp.x * RB, 16)
        sc.fin_b[...] = sc.acc_b[c, pl.ds(own, RB), :] + up(sc.bf_recv[c, 0]) + up(sc.bf_recv[c, 1])

    def drain(self):
        sc, c = self.sc, self.chunk
        sent = ((sc.h_recv, 0), (sc.f_recv, 1), (sc.bh_recv, 2), (sc.a_send, 3), (sc.b_send, 4), (sc.bf_recv, 5))
        for ref, kind in sent:
            self.sent(ref.at[c], kind)


class Refs:
    def __init__(self, **kw):
        self.__dict__.update(kw)


def scratch(width, hidden, modules, rows):
    bf, f32 = jnp.bfloat16, jnp.float32
    tokens = CHUNKS * CHUNK
    v = pltpu.VMEM
    return dict(
        xg=v((tokens, width), bf),
        og=v((tokens, width), bf),
        w_in=v((hidden, width), bf),
        w_out=v((hidden, width), bf),
        act=v((tokens, hidden), bf),
        slope=v((tokens, hidden), f32),
        pre_grad=v((tokens, hidden), bf),
        tgt=v((CHUNKS * OWN, width), bf),
        keep=v((CHUNKS * OWN, CHUNKS * OWN), f32),
        part=v((CHUNKS, 4, LINE, width), bf),
        h_recv=v((CHUNKS, 2, 4, RA, width // 2), bf),
        f_recv=v((CHUNKS, 2, 4, RA, width), bf),
        a_send=v((CHUNKS, 3, RA, width), bf),
        a_recv=v((CHUNKS, 5, RA, width), bf),
        b_send=v((CHUNKS, 3, SUPER, width), bf),
        b_recv=v((CHUNKS, 5, SUPER, width), bf),
        bh_send=v((CHUNKS, RB, width), bf),
        bh_recv=v((CHUNKS, 2, RB, width // 2), bf),
        bf_send=v((CHUNKS, 2, RB, width), bf),
        bf_recv=v((CHUNKS, 2, RB, width), bf),
        acc_a=v((CHUNKS, RA, width), f32),
        acc_b=v((CHUNKS, SUPER, width), f32),
        fin_b=v((RB, width), f32),
        g_send=pltpu.SemaphoreType.DMA((CHUNKS, 6)),
        g_recv=pltpu.SemaphoreType.DMA((CHUNKS, Gather.RECV)),
        rs_send=pltpu.SemaphoreType.DMA((CHUNKS, 6)),
        rs_recv=pltpu.SemaphoreType.DMA((CHUNKS, Reduce.RECV)),
        local=pltpu.SemaphoreType.DMA((5,)),
        own=pltpu.SemaphoreType.DMA((CHUNKS, 2)),
        d_send=v((2, 2, HALF, hidden, rows), bf),
        d_recv=v((2, 2, HALF, hidden, rows), bf),
        z_send=v((2, modules, hidden, rows), bf),
        z_recv=v((2, modules, hidden, rows), bf),
        fresh=v((2, modules, hidden, rows), bf),
        far_00=v((modules, SPLIT, rows), bf),
        far_01=v((modules, hidden - SPLIT, rows), bf),
        far_10=v((modules, SPLIT, rows), bf),
        far_11=v((modules, hidden - SPLIT, rows), bf),
        mast=v((2, modules, hidden, rows), f32),
        mom=v((2, modules, hidden, rows), f32),
        ds=pltpu.SemaphoreType.DMA((2, 2, PIECES)),
        dr=pltpu.SemaphoreType.DMA((2, 2, PIECES)),
        os=pltpu.SemaphoreType.DMA((2, 2, PIECES)),
        orv=pltpu.SemaphoreType.DMA((2, 2, PIECES)),
        own_out=pltpu.SemaphoreType.DMA((2, 2, PIECES)),
        zs=pltpu.SemaphoreType.DMA((2, 2, PIECES)),
        zr=pltpu.SemaphoreType.DMA((2, 2, PIECES)),
        out=pltpu.SemaphoreType.DMA((2, 2, PIECES)),
    )


HALF = 8
SPLIT = 128
PIECES = 2
PATHS_PER_MODULE = 4


class Group:
    def __init__(self):
        p = lax.axis_index("path")
        self.h, self.i = p // HALF, p % HALF
        self.y, self.c = self.i // 2, self.i % 2
        self.across = (1 - self.h) * HALF + self.i

    def peer(self, i):
        return self.h * HALF + i


def pcopy(src, dst, ssem, rsem, p):
    return pltpu.make_async_remote_copy(
        src_ref=src, dst_ref=dst, send_sem=ssem, recv_sem=rsem, device_id={"path": p}, device_id_type=MESH
    )


def path_phase(pg, sc, width_scale, hidden_scale, table, new_w, new_mast, new_mom):
    h, me = pg.h, pg.i
    hidden, rows = sc.mast.shape[2:]
    modules = sc.mast.shape[1]
    operands = ((sc.xg, sc.pre_grad, width_scale), (sc.og, sc.act, hidden_scale))

    def half(side):
        return h if side == 0 else 1 - h

    STEP = 32
    pieces = ((0, SPLIT), (SPLIT, hidden - SPLIT))

    def units(piece):
        return pl.ds(*pieces[piece])

    def dcopy(level, side, piece, i, src):
        return pcopy(
            sc.d_send.at[level, side, i, units(piece)],
            sc.d_recv.at[level, side, src, units(piece)],
            sc.ds.at[level, side, piece],
            sc.dr.at[level, side, piece],
            pg.peer(i),
        )

    def changes(level, side, which):
        left, right, scale = operands[level]
        first = pieces[which[0]][0]
        count = sum(pieces[piece][1] for piece in which)

        def run(k, c):
            d = jnp.where(k == 0, 2, jnp.where(k == 1, 1, jnp.where(k == 2, 3, 0)))
            y = (pg.y + d) % 4
            cols = pl.ds(pl.multiple_of((half(side) * HALF + 2 * y) * rows, 128), 2 * rows)
            g = lax.dot_general(
                right[:, first : first + count], left[:, cols], (((0,), (0,)), ((), ())), preferred_element_type=jnp.float32
            )
            g = (INNER_LR * scale * g).astype(jnp.bfloat16)
            for core in (0, 1):
                i = 2 * y + core
                part = g[:, core * rows : (core + 1) * rows]

                @pl.when(i == me)
                def _():
                    sc.d_recv[level, side, i, pl.ds(first, count), :] = part

                @pl.when(i != me)
                def _():
                    sc.d_send[level, side, i, pl.ds(first, count), :] = part
                    for piece in which:
                        dcopy(level, side, piece, i, me).start()

            return c

        lax.fori_loop(0, 4, run, 0)

    def all_dcopies(level, side, piece):
        ref = sc.d_recv.at[level, side, pl.ds(0, HALF - 1), units(piece)]
        return pcopy(ref, ref, sc.ds.at[level, side, piece], sc.dr.at[level, side, piece], pg.across)

    def await_changes(level, side, piece):
        all_dcopies(level, side, piece).wait_recv()

    def sums(level, side, piece, use):
        def run(k, c):
            part = pl.ds(pl.multiple_of(pieces[piece][0] + k * STEP, STEP), STEP)
            total = [jnp.zeros((STEP, rows), jnp.float32) for _ in range(modules)]
            for i in range(HALF):
                change = sc.d_recv[level, side, i, part, :].astype(jnp.float32)
                named = table[level, pg.peer(i)]
                for m in range(modules):
                    total[m] = total[m] + jnp.where(named == m, 1.0, 0.0) * change
            for m in range(modules):
                use(m, part, total[m])
            return c

        lax.fori_loop(0, pieces[piece][1] // STEP, run, 0)

    far = ((sc.far_00, sc.far_01), (sc.far_10, sc.far_11))

    def zcopy(kind, level, piece):
        src = (sc.z_send, sc.fresh)[kind].at[level, :, units(piece)]
        dst = far[level][piece] if kind else sc.z_recv.at[level, :, units(piece)]
        return pcopy(src, dst, sc.zs.at[kind, level, piece], sc.zr.at[kind, level, piece], pg.across)

    def sums_across(level, piece):
        await_changes(level, 1, piece)

        def use(m, part, total):
            sc.z_send[level, m, part, :] = total.astype(jnp.bfloat16)

        sums(level, 1, piece, use)
        zcopy(0, level, piece).start()

    def outs(level, piece):
        where = (level, slice(None), units(piece))
        return [
            pltpu.make_async_copy(sc.mast.at[where], new_mast.at[where], sc.out.at[0, level, piece]),
            pltpu.make_async_copy(sc.mom.at[where], new_mom.at[where], sc.out.at[1, level, piece]),
        ]

    def update(level, piece):
        await_changes(level, 0, piece)
        zcopy(0, level, piece).wait_recv()

        def use(m, part, total):
            average = (total + sc.z_recv[level, m, part, :].astype(jnp.float32)) * (1.0 / PATHS_PER_MODULE)
            moved = MOMENT * sc.mom[level, m, part, :] + average
            master = sc.mast[level, m, part, :] - OUTER_LR * (average + MOMENT * moved)
            sc.mom[level, m, part, :] = moved
            sc.mast[level, m, part, :] = master
            sc.fresh[level, m, part, :] = master.astype(jnp.bfloat16)

        sums(level, 0, piece, use)
        zcopy(1, level, piece).start()
        for c in outs(level, piece):
            c.start()

    def ocopy(level, side, piece, i, src):
        place = pl.ds(pl.multiple_of((half(side) * HALF + src) * rows, 128), rows)
        return pcopy(
            sc.d_send.at[level, side, i, units(piece)],
            new_w.at[level, units(piece), place],
            sc.os.at[level, side, piece],
            sc.orv.at[level, side, piece],
            pg.peer(i),
        )

    def own_copy(level, side, piece):
        place = pl.ds(pl.multiple_of((half(side) * HALF + me) * rows, 128), rows)
        return pltpu.make_async_copy(
            sc.d_send.at[level, side, me, units(piece)],
            new_w.at[level, units(piece), place],
            sc.own_out.at[level, side, piece],
        )

    def hand_back(level, side, piece):
        if side == 1:
            zcopy(1, level, piece).wait_recv()
        all_dcopies(level, side, piece).wait_send()

        def run(k, c):
            i = (me + 1 + k) % HALF
            named = table[level, pg.peer(i)]
            new = sc.fresh[level, named, units(piece), :] if side == 0 else far[level][piece][named]
            sc.d_send[level, side, i, units(piece), :] = new

            @pl.when(i != me)
            def _():
                ocopy(level, side, piece, i, me).start()

            @pl.when(i == me)
            def _():
                own_copy(level, side, piece).start()

            return c

        lax.fori_loop(0, HALF, run, 0)

    changes(1, 1, (0,))
    changes(1, 1, (1,))
    sums_across(1, 0)
    changes(0, 1, (1,))
    sums_across(1, 1)
    changes(0, 1, (0,))
    sums_across(0, 1)
    changes(1, 0, (0, 1))
    sums_across(0, 0)
    changes(0, 0, (0, 1))
    update(1, 0)
    update(1, 1)
    hand_back(1, 0, 0)
    hand_back(1, 0, 1)
    update(0, 1)
    update(0, 0)
    hand_back(1, 1, 0)
    hand_back(0, 0, 1)
    hand_back(0, 0, 0)
    hand_back(1, 1, 1)
    hand_back(0, 1, 1)
    hand_back(0, 1, 0)

    for level in (0, 1):
        for side in (0, 1):
            for piece in range(PIECES):
                own_copy(level, side, piece).wait()
                ref = sc.d_send.at[level, side, pl.ds(0, HALF - 1), units(piece)]
                others = pcopy(ref, ref, sc.os.at[level, side, piece], sc.orv.at[level, side, piece], pg.across)
                others.wait_recv()
                others.wait_send()
        for piece in range(PIECES):
            zcopy(0, level, piece).wait_send()
            zcopy(1, level, piece).wait_send()
            for c in outs(level, piece):
                c.wait()


def step_kernel(names, width_scale, hidden_scale, tokens, x_ref, t_ref, ids_ref, table_ref, w_ref, mast_ref, mom_ref,
                new_w_ref, new_mast_ref, new_mom_ref, *refs):
    sc = Refs(**dict(zip(names, refs)))
    pp = Place()
    pg = Group()
    x, z, w = pp.x, pp.z, pp.w
    own = [(c * OWN, rows_a(c, x, z), RA) for c in range(CHUNKS)] + [(c * OWN + RA, rows_b(c, x, z), RB) for c in range(CHUNKS)]

    mine = [
        pltpu.make_async_copy(x_ref.at[pl.ds(lo, n)], sc.xg.at[pl.ds(start, n)], sc.own.at[k // 2, k % 2])
        for k, (lo, start, n) in enumerate(own)
    ]
    loads = [
        pltpu.make_async_copy(w_ref.at[0], sc.w_in, sc.local.at[0]),
        pltpu.make_async_copy(w_ref.at[1], sc.w_out, sc.local.at[1]),
        pltpu.make_async_copy(t_ref, sc.tgt, sc.local.at[2]),
        pltpu.make_async_copy(mast_ref, sc.mast, sc.local.at[3]),
        pltpu.make_async_copy(mom_ref, sc.mom, sc.local.at[4]),
    ]
    for c in mine + loads:
        c.start()

    barrier = pltpu.get_barrier_semaphore()
    for f in (pp.right, pp.left, pp.inner):
        pl.semaphore_signal(barrier, inc=1, device_id={"fsdp": f}, device_id_type=MESH)

    @pl.when(w == 1)
    def _():
        pl.semaphore_signal(barrier, inc=1, device_id={"fsdp": pp.edge}, device_id_type=MESH)

    for i in range(HALF):

        @pl.when(pg.i != i)
        def _():
            pl.semaphore_signal(barrier, inc=1, device_id={"path": pg.peer(i)}, device_id_type=MESH)

    pl.semaphore_signal(barrier, inc=1, device_id={"path": pg.across}, device_id_type=MESH)
    pl.semaphore_wait(barrier, 3 + HALF + w)
    for c in mine + loads[:1]:
        c.wait()

    def across_width(rows, weights):
        return lax.dot_general(rows, weights[...], (((1,), (1,)), ((), ())), preferred_element_type=jnp.float32)

    def forward(start, n):
        rows = pl.ds(start, n)
        pre = across_width(sc.xg[rows, :], sc.w_in) * width_scale
        sig = jax.nn.sigmoid(pre)
        sc.act[rows, :] = (pre * sig).astype(jnp.bfloat16)
        sc.slope[rows, :] = sig * (1.0 + pre * (1.0 - sig))

    def partial(start, n, cs):
        return jnp.dot(sc.act[pl.ds(start, n), :], sc.w_out[:, cs], preferred_element_type=jnp.float32) * hidden_scale

    def loss_grad(total, lo, start, n):
        res = up(sc.xg[pl.ds(start, n), :]) + total - up(sc.tgt[pl.ds(lo, n), :])
        sc.og[pl.ds(start, n), :] = (sc.keep[pl.ds(lo, n), 0:1] * res / tokens).astype(jnp.bfloat16)

    def backward(start, n):
        rows = pl.ds(start, n)
        act_grad = across_width(sc.og[rows, :], sc.w_out) * hidden_scale
        sc.pre_grad[rows, :] = (act_grad * sc.slope[rows, :]).astype(jnp.bfloat16)

    first = [Gather(pp, c, sc.xg, sc.g_send, sc.g_recv, forward) for c in range(CHUNKS)]
    sums = [Reduce(pp, c, partial, sc) for c in range(CHUNKS)]
    second = [Gather(pp, c, sc.og, sc.g_send, sc.g_recv, backward) for c in range(CHUNKS)]

    def turn_over(c):
        sums[c].finish()
        loss_grad(sc.acc_a[c], *own[c])
        loss_grad(sc.fin_b[...], *own[CHUNKS + c])
        first[c].finish()
        second[c].start()

    def steps(*jobs):
        def run(k, carry):
            for job, offset in jobs:
                job.step(k + offset)
            return carry

        lax.fori_loop(0, STEPS // 2, run, 0)

    late = STEPS // 2
    first[0].start()
    steps((first[0], 0))
    first[1].start()
    steps((first[0], late), (first[1], 0))
    for c in loads[1:]:
        c.wait()
    kept = (ids_ref[...] >= SPECIAL).astype(jnp.float32)
    sc.keep[...] = jnp.broadcast_to(kept, sc.keep.shape).T
    steps((sums[0], 0), (first[1], late))
    steps((sums[0], late), (sums[1], 0))
    turn_over(0)
    steps((second[0], 0), (sums[1], late))
    turn_over(1)
    steps((second[0], late), (second[1], 0))
    steps((second[1], late))
    path_phase(pg, sc, width_scale, hidden_scale, table_ref, new_w_ref, new_mast_ref, new_mom_ref)
    for job in second:
        job.finish()
    for job in sums:
        job.drain()


def turn(v):
    return jnp.swapaxes(v, -1, -2)


def per_device(inputs, targets, token_ids, module_table, path_weights, master, momentum):
    width, hidden = path_weights.shape[2:]
    n = lax.axis_size("fsdp")
    tokens = inputs.shape[1] * n
    modules, rows = master.shape[1:3]
    spec = scratch(width, hidden, modules, rows)
    hbm = pl.BlockSpec(memory_space=pl.ANY)
    vmem = pl.BlockSpec(memory_space=pltpu.VMEM)
    smem = pl.BlockSpec(memory_space=pltpu.SMEM)
    new_weights, new_master, new_momentum = pl.pallas_call(
        functools.partial(step_kernel, tuple(spec), width ** (-0.5), (hidden * n) ** (-0.5), tokens),
        out_shape=(
            jax.ShapeDtypeStruct((2, hidden, width), jnp.bfloat16),
            jax.ShapeDtypeStruct((2, modules, hidden, rows), jnp.float32),
            jax.ShapeDtypeStruct((2, modules, hidden, rows), jnp.float32),
        ),
        in_specs=[hbm, hbm, vmem, smem, hbm, hbm, hbm],
        out_specs=(hbm, hbm, hbm),
        scratch_shapes=list(spec.values()),
        compiler_params=pltpu.CompilerParams(
            collective_id=0, has_side_effects=True, vmem_limit_bytes=63 * 1024 * 1024
        ),
        name="outer_step",
    )(inputs[0], targets[0], token_ids, module_table.T, turn(path_weights[0]), turn(master), turn(momentum))
    return (turn(new_weights)[None], turn(new_master), turn(new_momentum))


def solution(mesh):
    in_specs = (
        P("path", "fsdp", None),
        P("path", "fsdp", None),
        P("path", "fsdp"),
        P(),
        P("path", None, None, "fsdp"),
        P(None, None, "path", "fsdp"),
        P(None, None, "path", "fsdp"),
    )
    out_specs = (
        P("path", None, None, "fsdp"),
        P(None, None, "path", "fsdp"),
        P(None, None, "path", "fsdp"),
    )
    return jax.shard_map(
        per_device, mesh=mesh, in_specs=in_specs, out_specs=out_specs, check_vma=False
    )
```

```python
import functools

import jax
import jax.numpy as jnp
from jax import lax
from jax.experimental import pallas as pl
from jax.experimental.pallas import tpu as pltpu
from jax.sharding import PartitionSpec as P

SPECIAL = 256
INNER_LR = 4096.0
OUTER_LR = 0.7
MOMENT = 0.9
MESH = pl.DeviceIdType.MESH

CHUNKS = 2
RA, RB = 48, 16
NX, NZ = 4, 4
LINE = NX * RA
SUPER = NX * RB
ROWS_A = NZ * LINE
CHUNK = ROWS_A + NZ * SUPER
OWN = RA + RB


class Place:
    def __init__(self):
        f = lax.axis_index("fsdp")
        self.x, self.z = f // NZ, f % NZ
        self.far = self.z // 2
        self.w = (self.z + self.far) % 2
        flip = 1 - 2 * self.far
        self.flip = flip
        self.right = ((self.x + 1) % NX) * NZ + self.z
        self.left = ((self.x + NX - 1) % NX) * NZ + self.z
        self.inner = self.x * NZ + self.z + flip
        self.edge = self.x * NZ + self.z - flip

    def zb(self, r):
        swap = jnp.where(r == 0, 1, jnp.where(r == 1, -1, 0))
        o = r + self.w * swap
        return o * self.flip + (NZ - 1) * self.far

    def col(self, dx):
        return (self.x + dx + NX) % NX


def rows_line(c, z):
    return pl.multiple_of(c * CHUNK + z * LINE, 16)


def rows_a(c, x, z):
    return pl.multiple_of(c * CHUNK + z * LINE + x * RA, 16)


def rows_b(c, x, z):
    return pl.multiple_of(c * CHUNK + ROWS_A + z * SUPER + x * RB, 16)


def rows_super(c, z):
    return pl.multiple_of(c * CHUNK + ROWS_A + z * SUPER, 16)


def rcopy(src, dst, ssem, rsem, f):
    return pltpu.make_async_remote_copy(
        src_ref=src, dst_ref=dst, send_sem=ssem, recv_sem=rsem, device_id={"fsdp": f}, device_id_type=MESH
    )


STEPS = 6


class Gather:
    FIRST = (0, 4, 12, 20, 22, 24)
    PER_SIDE = (4, 4, 4, 1, 1, 4)
    RECV = 28

    def __init__(self, pp, chunk, buf, ssem, rsem, compute):
        self.pp, self.chunk, self.buf, self.ssem, self.rsem, self.compute = pp, chunk, buf, ssem, rsem, compute
        self.half = buf.shape[1] // 2

    def piece(self, start, n, side=None):
        if side is None:
            return self.buf.at[pl.ds(start, n)]
        return self.buf.at[pl.ds(start, n), pl.ds(side * self.half, self.half)]

    def copy(self, kind, side, i, ref, f, slot):
        c = self.chunk
        got = self.FIRST[kind] + slot[0] * self.PER_SIDE[kind] + slot[1]
        return rcopy(ref, ref, self.ssem.at[c, kind], self.rsem.at[c, got], f)

    def push(self, kind, side, i, ref, f, slot):
        self.copy(kind, side, i, ref, f, slot).start()

    def arrived(self, kind, side, i, ref):
        self.copy(kind, side, i, ref, self.pp.right, (side, i)).wait_recv()

    def sent(self, kind, n):
        self.copy(kind, 0, 0, self.piece(0, n), self.pp.right, (0, 0)).wait_send()

    def z_own(self, kind, ref):
        pp = self.pp
        self.push(kind, 0, 0, ref, pp.inner, (0, pp.z))

        @pl.when(pp.w == 1)
        def _():
            self.push(kind, 1, 0, ref, pp.edge, (0, pp.z))

    def z_forward(self, kind, r, zb, ref):
        pp = self.pp

        @pl.when((pp.w == 1) & (r == 1))
        def _():
            self.push(kind, 0, r, ref, pp.inner, (0, zb))

        @pl.when((pp.w == 1) & (r >= 2))
        def _():
            self.push(kind, 1, r, ref, pp.edge, (0, zb))

    def start(self):
        pp, c = self.pp, self.chunk
        self.z_own(0, self.piece(rows_a(c, pp.x, pp.z), RA))
        for side, f in ((0, pp.right), (1, pp.left)):
            self.push(3, side, 0, self.piece(rows_b(c, pp.x, pp.z), RB), f, (side, 0))

    def step(self, t):
        pp, c = self.pp, self.chunk
        z = pp.z
        sides = ((0, -1, pp.right), (1, 1, pp.left))
        zt, zl = pp.zb(t), pp.zb(t - 1)

        @pl.when((t >= 1) & (t <= 3))
        def _():
            ref = self.piece(rows_a(c, pp.x, zt), RA)
            self.arrived(0, 0, zt, ref)
            self.z_forward(0, t, zt, ref)

        @pl.when(t <= 3)
        def _():
            for side, _, f in sides:
                self.push(1, side, t, self.piece(rows_a(c, pp.x, zt), RA), f, (side, t))

        @pl.when(t == 0)
        def _():
            for side, dx, f in sides:
                start = rows_b(c, pp.col(dx), z)
                self.arrived(3, side, 0, self.piece(start, RB))
                self.push(4, side, 0, self.piece(start, RB, side), f, (side, 0))

        @pl.when((t >= 1) & (t <= 4))
        def _():
            for side, dx, f in sides:
                start = rows_a(c, pp.col(dx), zl)
                self.arrived(1, side, t - 1, self.piece(start, RA))
                self.push(2, side, t - 1, self.piece(start, RA, side), f, (side, t - 1))

        @pl.when(t == 1)
        def _():
            for side in (0, 1):
                self.arrived(4, side, 0, self.piece(rows_b(c, pp.col(2), z), RB, side))
            self.z_own(5, self.piece(rows_super(c, z), SUPER))

        @pl.when((t >= 2) & (t <= 4))
        def _():
            ref = self.piece(rows_super(c, zl), SUPER)
            self.arrived(5, 0, zl, ref)
            self.z_forward(5, t - 1, zl, ref)

        @pl.when(t >= 2)
        def _():
            zo = pp.zb(t - 2)
            for side in (0, 1):
                self.arrived(2, side, t - 2, self.piece(rows_a(c, pp.col(2), zo), RA, side))

    def work(self, t):
        pp, c = self.pp, self.chunk

        @pl.when((t >= 1) & (t <= 4))
        def _():
            self.compute(rows_super(c, pp.zb(t - 1)), SUPER)

        @pl.when(t >= 2)
        def _():
            self.compute(rows_line(c, pp.zb(t - 2)), LINE)

    def finish(self):
        for kind, n in ((0, RA), (5, SUPER)):

            @pl.when(self.pp.w == 0)
            def _():
                self.sent(kind, n)

            @pl.when(self.pp.w == 1)
            def _():
                self.sent(kind, 5 * n)

        for kind, n in ((1, 8 * RA), (2, 4 * RA), (3, 2 * RB), (4, RB)):
            self.sent(kind, n)


COLS = 512


def up(v):
    return v.astype(jnp.float32)


class Reduce:
    def __init__(self, pp, chunk, partial, sc):
        self.pp, self.chunk, self.partial, self.sc = pp, chunk, partial, sc
        self.width = sc.acc_a.shape[-1]

    def over(self, body, first=0, width=None):
        def run(k, carry):
            body(pl.ds(pl.multiple_of(first + k * COLS, 128), COLS))
            return carry

        lax.fori_loop(0, (width or self.width) // COLS, run, 0)

    FIRST = (0, 8, 16, 18, 23, 28)
    PER_SIDE = (4, 4, 1, 5, 5, 1)
    RECV = 30

    def copy(self, src, dst, kind, side, i, f, slot):
        c, sc = self.chunk, self.sc
        got = self.FIRST[kind] + slot[0] * self.PER_SIDE[kind] + slot[1]
        return rcopy(src, dst, sc.rs_send.at[c, kind], sc.rs_recv.at[c, got], f)

    def push(self, src, dst, kind, side, i, f, slot):
        self.copy(src, dst, kind, side, i, f, slot).start()

    def arrived(self, ref, kind, side, i):
        self.copy(ref, ref, kind, side, i, self.pp.right, (side, i)).wait_recv()

    def sent(self, ref, kind):
        self.copy(ref, ref, kind, 0, 0, self.pp.right, (0, 0)).wait_send()

    def z_stage(self, kind, r, acc, recv, send):
        pp, c, w = self.pp, self.chunk, self.pp.w

        @pl.when((w == 1) & (r >= 1))
        def _():
            self.arrived(recv.at[c, r], kind, 0, r)

            def add(cs):
                send[c, r - 1, :, cs] = (acc[c, :, cs] + up(recv[c, r, :, cs])).astype(jnp.bfloat16)

            self.over(add)

        @pl.when((w == 1) & (r >= 2))
        def _():
            slot = jnp.where(r == 3, 1, 0)
            self.push(send.at[c, r - 1], recv.at[c, slot], kind, 0, r, pp.inner, (0, slot))

        @pl.when((w == 1) & (r == 1))
        def _():
            self.push(send.at[c, r - 1], recv.at[c, 0], kind, 0, r, pp.edge, (0, 0))

        @pl.when((w == 0) & (r >= 1))
        def _():
            def cast(cs):
                send[c, r - 1, :, cs] = acc[c, :, cs].astype(jnp.bfloat16)

            self.over(cast)
            slot = jnp.where(r == 1, 4, r)
            self.push(send.at[c, r - 1], recv.at[c, slot], kind, 0, r, pp.inner, (0, slot))

        def last(i):
            self.arrived(recv.at[c, i], kind, 0, i)

            def add(cs):
                acc[c, :, cs] = acc[c, :, cs] + up(recv[c, i, :, cs])

            self.over(add)

        @pl.when(r == 0)
        def _():
            last(0)

        @pl.when((w == 1) & (r == 0))
        def _():
            last(4)

    def b_round(self, r):
        sc, c = self.sc, self.chunk
        start = rows_super(c, self.pp.zb(r))

        def fill(cs):
            sc.acc_b[c, :, cs] = self.partial(start, SUPER, cs)

        self.over(fill)
        self.z_stage(4, r, sc.acc_b, sc.b_recv, sc.b_send)

    def fill(self, r):
        sc, c = self.sc, self.chunk
        start = rows_line(c, self.pp.zb(r))

        def body(cs):
            sc.part[c, r, :, cs] = self.partial(start, LINE, cs).astype(jnp.bfloat16)

        self.over(body)

    def start(self):
        self.fill(3)

    def work(self, t):
        @pl.when(t <= 2)
        def _():
            self.fill(2 - t)

    def step(self, t):
        pp, sc, c, w = self.pp, self.sc, self.chunk, self.pp.w
        r0, r1, r2 = 3 - t, 4 - t, 5 - t
        half = self.width // 2

        def rows(dx, n):
            return pl.ds(pl.multiple_of(pp.col(dx) * n, 16), n)

        sides = ((0, 1, pp.right, half), (1, -1, pp.left, 0))

        @pl.when(t <= 3)
        def _():
            for side, _, f, lo in sides:
                src = sc.part.at[c, r0, rows(2, RA), pl.ds(lo, half)]
                self.push(src, sc.h_recv.at[c, side, r0], 0, side, r0, f, (side, r0))

        @pl.when((t == 0) & (w == 0))
        def _():
            def run(i, carry):
                self.b_round(3 - i)
                return carry

            lax.fori_loop(0, 3, run, 0)

        @pl.when((t >= 1) & (t <= 4))
        def _():
            for side, dx, f, lo in sides:
                self.arrived(sc.h_recv.at[c, side, r1], 0, side, r1)
                where = rows(dx, RA)

                def add(cs):
                    to = pl.ds(pl.multiple_of(lo + cs.start, 128), COLS)
                    sc.part[c, r1, where, to] = (up(sc.part[c, r1, where, to]) + up(sc.h_recv[c, side, r1, :, cs])).astype(jnp.bfloat16)

                self.over(add, width=half)
                self.push(sc.part.at[c, r1, where], sc.f_recv.at[c, side, r1], 1, side, r1, f, (side, r1))

        @pl.when((t >= 1) & (t <= 3) & (w == 1))
        def _():
            self.b_round(r1)

        @pl.when(t == 4)
        def _():
            self.b_round(0)
            sc.bh_send[c] = sc.acc_b[c, rows(2, RB), :].astype(jnp.bfloat16)
            for side, _, f, lo in sides:
                self.push(sc.bh_send.at[c, :, pl.ds(lo, half)], sc.bh_recv.at[c, side], 2, side, 0, f, (side, 0))

        @pl.when(t >= 2)
        def _():
            for side in (0, 1):
                self.arrived(sc.f_recv.at[c, side, r2], 1, side, r2)
            where = rows(0, RA)

            def fill(cs):
                sc.acc_a[c, :, cs] = up(sc.part[c, r2, where, cs]) + up(sc.f_recv[c, 0, r2, :, cs]) + up(sc.f_recv[c, 1, r2, :, cs])

            self.over(fill)
            self.z_stage(3, r2, sc.acc_a, sc.a_recv, sc.a_send)

        @pl.when(t == 4)
        def _():
            for side, dx, f, lo in sides:
                self.arrived(sc.bh_recv.at[c, side], 2, side, 0)
                where = rows(dx, RB)
                got, alone = pl.ds(lo, half), pl.ds(half - lo, half)
                sc.bf_send[c, side, :, got] = (sc.acc_b[c, where, got] + up(sc.bh_recv[c, side])).astype(jnp.bfloat16)
                sc.bf_send[c, side, :, alone] = sc.acc_b[c, where, alone].astype(jnp.bfloat16)
                self.push(sc.bf_send.at[c, side], sc.bf_recv.at[c, side], 5, side, 0, f, (side, 0))

    def finish(self):
        pp, sc, c = self.pp, self.sc, self.chunk
        for side in (0, 1):
            self.arrived(sc.bf_recv.at[c, side], 5, side, 0)
        own = pl.multiple_of(pp.x * RB, 16)
        sc.fin_b[...] = sc.acc_b[c, pl.ds(own, RB), :] + up(sc.bf_recv[c, 0]) + up(sc.bf_recv[c, 1])

    def drain(self):
        sc, c = self.sc, self.chunk
        sent = ((sc.h_recv, 0), (sc.f_recv, 1), (sc.bh_recv, 2), (sc.a_send, 3), (sc.b_send, 4), (sc.bf_recv, 5))
        for ref, kind in sent:
            self.sent(ref.at[c], kind)


class Refs:
    def __init__(self, **kw):
        self.__dict__.update(kw)


def scratch(width, hidden, modules, rows):
    bf, f32 = jnp.bfloat16, jnp.float32
    tokens = CHUNKS * CHUNK
    v = pltpu.VMEM
    return dict(
        xg=v((tokens, width), bf),
        og=v((tokens, width), bf),
        w_in=v((hidden, width), bf),
        w_out=v((hidden, width), bf),
        act=v((tokens, hidden), bf),
        slope=v((tokens, hidden), f32),
        pre_grad=v((tokens, hidden), bf),
        tgt=v((CHUNKS * OWN, width), bf),
        keep=v((CHUNKS * OWN, CHUNKS * OWN), f32),
        part=v((CHUNKS, 4, LINE, width), bf),
        h_recv=v((CHUNKS, 2, 4, RA, width // 2), bf),
        f_recv=v((CHUNKS, 2, 4, RA, width), bf),
        a_send=v((CHUNKS, 3, RA, width), bf),
        a_recv=v((CHUNKS, 5, RA, width), bf),
        b_send=v((CHUNKS, 3, SUPER, width), bf),
        b_recv=v((CHUNKS, 5, SUPER, width), bf),
        bh_send=v((CHUNKS, RB, width), bf),
        bh_recv=v((CHUNKS, 2, RB, width // 2), bf),
        bf_send=v((CHUNKS, 2, RB, width), bf),
        bf_recv=v((CHUNKS, 2, RB, width), bf),
        acc_a=v((CHUNKS, RA, width), f32),
        acc_b=v((CHUNKS, SUPER, width), f32),
        fin_b=v((RB, width), f32),
        g_send=pltpu.SemaphoreType.DMA((CHUNKS, 6)),
        g_recv=pltpu.SemaphoreType.DMA((CHUNKS, Gather.RECV)),
        rs_send=pltpu.SemaphoreType.DMA((CHUNKS, 6)),
        rs_recv=pltpu.SemaphoreType.DMA((CHUNKS, Reduce.RECV)),
        local=pltpu.SemaphoreType.DMA((5,)),
        own=pltpu.SemaphoreType.DMA((CHUNKS, 2)),
        d_send=v((2, 2, HALF, hidden, rows), bf),
        d_recv=v((2, 2, HALF, hidden, rows), bf),
        z_send=v((2, modules, hidden, rows), bf),
        z_recv=v((2, modules, hidden, rows), bf),
        fresh=v((2, modules, hidden, rows), bf),
        far_00=v((modules, SPLIT, rows), bf),
        far_01=v((modules, hidden - SPLIT, rows), bf),
        far_10=v((modules, SPLIT, rows), bf),
        far_11=v((modules, hidden - SPLIT, rows), bf),
        mast=v((2, modules, hidden, rows), f32),
        mom=v((2, modules, hidden, rows), f32),
        ds=pltpu.SemaphoreType.DMA((2, 2, PIECES)),
        dr=pltpu.SemaphoreType.DMA((2, 2, PIECES)),
        os=pltpu.SemaphoreType.DMA((2, 2, PIECES)),
        orv=pltpu.SemaphoreType.DMA((2, 2, PIECES)),
        own_out=pltpu.SemaphoreType.DMA((2, 2, PIECES)),
        zs=pltpu.SemaphoreType.DMA((2, 2, PIECES)),
        zr=pltpu.SemaphoreType.DMA((2, 2, PIECES)),
        out=pltpu.SemaphoreType.DMA((2, 2, PIECES)),
    )


HALF = 8
SPLIT = 128
PIECES = 2
PATHS_PER_MODULE = 4


class Group:
    def __init__(self):
        p = lax.axis_index("path")
        self.h, self.i = p // HALF, p % HALF
        self.y, self.c = self.i // 2, self.i % 2
        self.across = (1 - self.h) * HALF + self.i

    def peer(self, i):
        return self.h * HALF + i


def pcopy(src, dst, ssem, rsem, p):
    return pltpu.make_async_remote_copy(
        src_ref=src, dst_ref=dst, send_sem=ssem, recv_sem=rsem, device_id={"path": p}, device_id_type=MESH
    )


def path_phase(pg, sc, width_scale, hidden_scale, table, new_w, new_mast, new_mom):
    h, me = pg.h, pg.i
    hidden, rows = sc.mast.shape[2:]
    modules = sc.mast.shape[1]
    operands = ((sc.xg, sc.pre_grad, width_scale), (sc.og, sc.act, hidden_scale))

    def half(side):
        return h if side == 0 else 1 - h

    STEP = 32
    pieces = ((0, SPLIT), (SPLIT, hidden - SPLIT))

    def units(piece):
        return pl.ds(*pieces[piece])

    def dcopy(level, side, piece, i, src):
        return pcopy(
            sc.d_send.at[level, side, i, units(piece)],
            sc.d_recv.at[level, side, src, units(piece)],
            sc.ds.at[level, side, piece],
            sc.dr.at[level, side, piece],
            pg.peer(i),
        )

    def changes(level, side, which):
        left, right, scale = operands[level]
        first = pieces[which[0]][0]
        count = sum(pieces[piece][1] for piece in which)

        def run(k, c):
            d = jnp.where(k == 0, 2, jnp.where(k == 1, 1, jnp.where(k == 2, 3, 0)))
            y = (pg.y + d) % 4
            cols = pl.ds(pl.multiple_of((half(side) * HALF + 2 * y) * rows, 128), 2 * rows)
            g = lax.dot_general(
                right[:, first : first + count], left[:, cols], (((0,), (0,)), ((), ())), preferred_element_type=jnp.float32
            )
            g = (INNER_LR * scale * g).astype(jnp.bfloat16)
            for core in (0, 1):
                i = 2 * y + core
                part = g[:, core * rows : (core + 1) * rows]

                @pl.when(i == me)
                def _():
                    sc.d_recv[level, side, i, pl.ds(first, count), :] = part

                @pl.when(i != me)
                def _():
                    sc.d_send[level, side, i, pl.ds(first, count), :] = part
                    for piece in which:
                        dcopy(level, side, piece, i, me).start()

            return c

        lax.fori_loop(0, 4, run, 0)

    def all_dcopies(level, side, piece):
        ref = sc.d_recv.at[level, side, pl.ds(0, HALF - 1), units(piece)]
        return pcopy(ref, ref, sc.ds.at[level, side, piece], sc.dr.at[level, side, piece], pg.across)

    def await_changes(level, side, piece):
        all_dcopies(level, side, piece).wait_recv()

    def sums(level, side, piece, use):
        def run(k, c):
            part = pl.ds(pl.multiple_of(pieces[piece][0] + k * STEP, STEP), STEP)
            total = [jnp.zeros((STEP, rows), jnp.float32) for _ in range(modules)]
            for i in range(HALF):
                change = sc.d_recv[level, side, i, part, :].astype(jnp.float32)
                named = table[level, pg.peer(i)]
                for m in range(modules):
                    total[m] = total[m] + jnp.where(named == m, 1.0, 0.0) * change
            for m in range(modules):
                use(m, part, total[m])
            return c

        lax.fori_loop(0, pieces[piece][1] // STEP, run, 0)

    far = ((sc.far_00, sc.far_01), (sc.far_10, sc.far_11))

    def zcopy(kind, level, piece):
        src = (sc.z_send, sc.fresh)[kind].at[level, :, units(piece)]
        dst = far[level][piece] if kind else sc.z_recv.at[level, :, units(piece)]
        return pcopy(src, dst, sc.zs.at[kind, level, piece], sc.zr.at[kind, level, piece], pg.across)

    def sums_across(level, piece):
        await_changes(level, 1, piece)

        def use(m, part, total):
            sc.z_send[level, m, part, :] = total.astype(jnp.bfloat16)

        sums(level, 1, piece, use)
        zcopy(0, level, piece).start()

    def outs(level, piece):
        where = (level, slice(None), units(piece))
        return [
            pltpu.make_async_copy(sc.mast.at[where], new_mast.at[where], sc.out.at[0, level, piece]),
            pltpu.make_async_copy(sc.mom.at[where], new_mom.at[where], sc.out.at[1, level, piece]),
        ]

    def update(level, piece):
        await_changes(level, 0, piece)
        zcopy(0, level, piece).wait_recv()

        def use(m, part, total):
            average = (total + sc.z_recv[level, m, part, :].astype(jnp.float32)) * (1.0 / PATHS_PER_MODULE)
            moved = MOMENT * sc.mom[level, m, part, :] + average
            master = sc.mast[level, m, part, :] - OUTER_LR * (average + MOMENT * moved)
            sc.mom[level, m, part, :] = moved
            sc.mast[level, m, part, :] = master
            sc.fresh[level, m, part, :] = master.astype(jnp.bfloat16)

        sums(level, 0, piece, use)
        zcopy(1, level, piece).start()
        for c in outs(level, piece):
            c.start()

    def ocopy(level, side, piece, i, src):
        place = pl.ds(pl.multiple_of((half(side) * HALF + src) * rows, 128), rows)
        return pcopy(
            sc.d_send.at[level, side, i, units(piece)],
            new_w.at[level, units(piece), place],
            sc.os.at[level, side, piece],
            sc.orv.at[level, side, piece],
            pg.peer(i),
        )

    def own_copy(level, side, piece):
        place = pl.ds(pl.multiple_of((half(side) * HALF + me) * rows, 128), rows)
        return pltpu.make_async_copy(
            sc.d_send.at[level, side, me, units(piece)],
            new_w.at[level, units(piece), place],
            sc.own_out.at[level, side, piece],
        )

    def hand_back(level, side, piece):
        if side == 1:
            zcopy(1, level, piece).wait_recv()
        all_dcopies(level, side, piece).wait_send()

        def run(k, c):
            i = (me + 1 + k) % HALF
            named = table[level, pg.peer(i)]
            new = sc.fresh[level, named, units(piece), :] if side == 0 else far[level][piece][named]
            sc.d_send[level, side, i, units(piece), :] = new

            @pl.when(i != me)
            def _():
                ocopy(level, side, piece, i, me).start()

            @pl.when(i == me)
            def _():
                own_copy(level, side, piece).start()

            return c

        lax.fori_loop(0, HALF, run, 0)

    changes(1, 1, (0,))
    changes(1, 1, (1,))
    sums_across(1, 0)
    changes(0, 1, (1,))
    sums_across(1, 1)
    changes(0, 1, (0,))
    sums_across(0, 1)
    changes(1, 0, (0, 1))
    sums_across(0, 0)
    changes(0, 0, (0, 1))
    update(1, 0)
    update(1, 1)
    hand_back(1, 0, 0)
    hand_back(1, 0, 1)
    update(0, 1)
    update(0, 0)
    hand_back(1, 1, 0)
    hand_back(0, 0, 1)
    hand_back(0, 0, 0)
    hand_back(1, 1, 1)
    hand_back(0, 1, 1)
    hand_back(0, 1, 0)

    for level in (0, 1):
        for side in (0, 1):
            for piece in range(PIECES):
                own_copy(level, side, piece).wait()
                ref = sc.d_send.at[level, side, pl.ds(0, HALF - 1), units(piece)]
                others = pcopy(ref, ref, sc.os.at[level, side, piece], sc.orv.at[level, side, piece], pg.across)
                others.wait_recv()
                others.wait_send()
        for piece in range(PIECES):
            zcopy(0, level, piece).wait_send()
            zcopy(1, level, piece).wait_send()
            for c in outs(level, piece):
                c.wait()


def step_kernel(names, width_scale, hidden_scale, tokens, x_ref, t_ref, ids_ref, table_ref, w_ref, mast_ref, mom_ref,
                new_w_ref, new_mast_ref, new_mom_ref, *refs):
    sc = Refs(**dict(zip(names, refs)))
    pp = Place()
    pg = Group()
    x, z, w = pp.x, pp.z, pp.w
    own = [(c * OWN, rows_a(c, x, z), RA) for c in range(CHUNKS)] + [(c * OWN + RA, rows_b(c, x, z), RB) for c in range(CHUNKS)]

    mine = [
        pltpu.make_async_copy(x_ref.at[pl.ds(lo, n)], sc.xg.at[pl.ds(start, n)], sc.own.at[k // 2, k % 2])
        for k, (lo, start, n) in enumerate(own)
    ]
    loads = [
        pltpu.make_async_copy(w_ref.at[0], sc.w_in, sc.local.at[0]),
        pltpu.make_async_copy(w_ref.at[1], sc.w_out, sc.local.at[1]),
        pltpu.make_async_copy(t_ref, sc.tgt, sc.local.at[2]),
        pltpu.make_async_copy(mast_ref, sc.mast, sc.local.at[3]),
        pltpu.make_async_copy(mom_ref, sc.mom, sc.local.at[4]),
    ]
    for c in mine + loads:
        c.start()

    barrier = pltpu.get_barrier_semaphore()
    for f in (pp.right, pp.left, pp.inner):
        pl.semaphore_signal(barrier, inc=1, device_id={"fsdp": f}, device_id_type=MESH)

    @pl.when(w == 1)
    def _():
        pl.semaphore_signal(barrier, inc=1, device_id={"fsdp": pp.edge}, device_id_type=MESH)

    for i in range(HALF):

        @pl.when(pg.i != i)
        def _():
            pl.semaphore_signal(barrier, inc=1, device_id={"path": pg.peer(i)}, device_id_type=MESH)

    pl.semaphore_signal(barrier, inc=1, device_id={"path": pg.across}, device_id_type=MESH)
    pl.semaphore_wait(barrier, 3 + HALF + w)
    for c in mine + loads[:1]:
        c.wait()

    def across_width(rows, weights):
        return lax.dot_general(rows, weights[...], (((1,), (1,)), ((), ())), preferred_element_type=jnp.float32)

    def forward(start, n):
        rows = pl.ds(start, n)
        pre = across_width(sc.xg[rows, :], sc.w_in) * width_scale
        sig = jax.nn.sigmoid(pre)
        sc.act[rows, :] = (pre * sig).astype(jnp.bfloat16)
        sc.slope[rows, :] = sig * (1.0 + pre * (1.0 - sig))

    def partial(start, n, cs):
        return jnp.dot(sc.act[pl.ds(start, n), :], sc.w_out[:, cs], preferred_element_type=jnp.float32) * hidden_scale

    def loss_grad(total, lo, start, n):
        res = up(sc.xg[pl.ds(start, n), :]) + total - up(sc.tgt[pl.ds(lo, n), :])
        sc.og[pl.ds(start, n), :] = (sc.keep[pl.ds(lo, n), 0:1] * res / tokens).astype(jnp.bfloat16)

    def backward(start, n):
        rows = pl.ds(start, n)
        act_grad = across_width(sc.og[rows, :], sc.w_out) * hidden_scale
        sc.pre_grad[rows, :] = (act_grad * sc.slope[rows, :]).astype(jnp.bfloat16)

    first = [Gather(pp, c, sc.xg, sc.g_send, sc.g_recv, forward) for c in range(CHUNKS)]
    sums = [Reduce(pp, c, partial, sc) for c in range(CHUNKS)]
    second = [Gather(pp, c, sc.og, sc.g_send, sc.g_recv, backward) for c in range(CHUNKS)]

    def turn_over(c):
        sums[c].finish()
        loss_grad(sc.acc_a[c], *own[c])
        loss_grad(sc.fin_b[...], *own[CHUNKS + c])
        first[c].finish()
        second[c].start()

    def steps(*jobs):
        def run(k, carry):
            for job, offset in jobs:
                job.step(k + offset)
            for job, offset in jobs:
                job.work(k + offset)
            return carry

        lax.fori_loop(0, STEPS // 2, run, 0)

    late = STEPS // 2
    first[0].start()
    steps((first[0], 0))
    first[1].start()
    steps((first[0], late), (first[1], 0))
    for c in loads[1:]:
        c.wait()
    kept = (ids_ref[...] >= SPECIAL).astype(jnp.float32)
    sc.keep[...] = jnp.broadcast_to(kept, sc.keep.shape).T
    sums[0].start()
    steps((sums[0], 0), (first[1], late))
    sums[1].start()
    steps((sums[0], late), (sums[1], 0))
    turn_over(0)
    steps((second[0], 0), (sums[1], late))
    turn_over(1)
    steps((second[0], late), (second[1], 0))
    steps((second[1], late))
    path_phase(pg, sc, width_scale, hidden_scale, table_ref, new_w_ref, new_mast_ref, new_mom_ref)
    for job in second:
        job.finish()
    for job in sums:
        job.drain()


LANES = 4


def land_kernel(*refs):
    count = (len(refs) - 2) // 3
    sems_in, sems_out = refs[-2:]
    ins, outs = [], []
    for k in range(count):
        src, dst, stage = refs[k], refs[count + k], refs[2 * count + k]
        size = src.shape[-2] // LANES // 16 * 16
        for lane in range(LANES):
            n = size if lane < LANES - 1 else src.shape[-2] - lane * size
            where = (slice(None),) * (len(src.shape) - 2) + (pl.ds(lane * size, n),)
            ins.append(pltpu.make_async_copy(src.at[where], stage.at[where], sems_in.at[k, lane]))
            outs.append(pltpu.make_async_copy(stage.at[where], dst.at[where], sems_out.at[k, lane]))
    for c in ins:
        c.start()
    for got, put in zip(ins, outs):
        got.wait()
        put.start()
    for c in outs:
        c.wait()


def land(*arrays):
    hbm = pl.BlockSpec(memory_space=pl.ANY)
    return pl.pallas_call(
        land_kernel,
        out_shape=tuple(jax.ShapeDtypeStruct(v.shape, v.dtype) for v in arrays),
        in_specs=[hbm] * len(arrays),
        out_specs=(hbm,) * len(arrays),
        scratch_shapes=[pltpu.VMEM(v.shape, v.dtype) for v in arrays] + [pltpu.SemaphoreType.DMA((len(arrays), LANES))] * 2,
        compiler_params=pltpu.CompilerParams(vmem_limit_bytes=60 * 1024 * 1024),
        name="land",
    )(*arrays)


def turn(v):
    return jnp.swapaxes(v, -1, -2)


def per_device(inputs, targets, token_ids, module_table, path_weights, master, momentum):
    width, hidden = path_weights.shape[2:]
    n = lax.axis_size("fsdp")
    tokens = inputs.shape[1] * n
    modules, rows = master.shape[1:3]
    spec = scratch(width, hidden, modules, rows)
    hbm = pl.BlockSpec(memory_space=pl.ANY)
    vmem = pl.BlockSpec(memory_space=pltpu.VMEM)
    smem = pl.BlockSpec(memory_space=pltpu.SMEM)
    new_weights, new_master, new_momentum = pl.pallas_call(
        functools.partial(step_kernel, tuple(spec), width ** (-0.5), (hidden * n) ** (-0.5), tokens),
        out_shape=(
            jax.ShapeDtypeStruct((2, hidden, width), jnp.bfloat16),
            jax.ShapeDtypeStruct((2, modules, hidden, rows), jnp.float32),
            jax.ShapeDtypeStruct((2, modules, hidden, rows), jnp.float32),
        ),
        in_specs=[hbm, hbm, vmem, smem, hbm, hbm, hbm],
        out_specs=(hbm, hbm, hbm),
        scratch_shapes=list(spec.values()),
        compiler_params=pltpu.CompilerParams(
            collective_id=0, has_side_effects=True, vmem_limit_bytes=63 * 1024 * 1024
        ),
        name="outer_step",
    )(inputs[0], targets[0], token_ids, module_table.T, turn(path_weights[0]), turn(master), turn(momentum))
    new_weights, new_master, new_momentum = land(new_weights, new_master, new_momentum)
    return (turn(new_weights)[None], turn(new_master), turn(new_momentum))


def solution(mesh):
    in_specs = (
        P("path", "fsdp", None),
        P("path", "fsdp", None),
        P("path", "fsdp"),
        P(),
        P("path", None, None, "fsdp"),
        P(None, None, "path", "fsdp"),
        P(None, None, "path", "fsdp"),
    )
    out_specs = (
        P("path", None, None, "fsdp"),
        P(None, None, "path", "fsdp"),
        P(None, None, "path", "fsdp"),
    )
    return jax.shard_map(
        per_device, mesh=mesh, in_specs=in_specs, out_specs=out_specs, check_vma=False
    )
```

```python
import functools

import jax
import jax.numpy as jnp
from jax import lax
from jax.experimental import pallas as pl
from jax.experimental.pallas import tpu as pltpu
from jax.sharding import PartitionSpec as P

SPECIAL = 256
INNER_LR = 4096.0
OUTER_LR = 0.7
MOMENT = 0.9
MESH = pl.DeviceIdType.MESH

CHUNKS = 2
RA, RB = 48, 16
NX, NZ = 4, 4
LINE = NX * RA
SUPER = NX * RB
ROWS_A = NZ * LINE
CHUNK = ROWS_A + NZ * SUPER
OWN = RA + RB


class Place:
    def __init__(self):
        f = lax.axis_index("fsdp")
        self.x, self.z = f // NZ, f % NZ
        self.far = self.z // 2
        self.w = (self.z + self.far) % 2
        flip = 1 - 2 * self.far
        self.flip = flip
        self.right = ((self.x + 1) % NX) * NZ + self.z
        self.left = ((self.x + NX - 1) % NX) * NZ + self.z
        self.inner = self.x * NZ + self.z + flip
        self.edge = self.x * NZ + self.z - flip

    def zb(self, r):
        swap = jnp.where(r == 0, 1, jnp.where(r == 1, -1, 0))
        o = r + self.w * swap
        return o * self.flip + (NZ - 1) * self.far

    def col(self, dx):
        return (self.x + dx + NX) % NX


def rows_line(c, z):
    return pl.multiple_of(c * CHUNK + z * LINE, 16)


def rows_a(c, x, z):
    return pl.multiple_of(c * CHUNK + z * LINE + x * RA, 16)


def rows_b(c, x, z):
    return pl.multiple_of(c * CHUNK + ROWS_A + z * SUPER + x * RB, 16)


def rows_super(c, z):
    return pl.multiple_of(c * CHUNK + ROWS_A + z * SUPER, 16)


def rcopy(src, dst, ssem, rsem, f):
    return pltpu.make_async_remote_copy(
        src_ref=src, dst_ref=dst, send_sem=ssem, recv_sem=rsem, device_id={"fsdp": f}, device_id_type=MESH
    )


STEPS = 6


class Gather:
    FIRST = (0, 4, 12, 20, 22, 24)
    PER_SIDE = (4, 4, 4, 1, 1, 4)
    RECV = 28

    def __init__(self, pp, chunk, buf, ssem, rsem, compute):
        self.pp, self.chunk, self.buf, self.ssem, self.rsem, self.compute = pp, chunk, buf, ssem, rsem, compute
        self.half = buf.shape[1] // 2

    def piece(self, start, n, side=None):
        if side is None:
            return self.buf.at[pl.ds(start, n)]
        return self.buf.at[pl.ds(start, n), pl.ds(side * self.half, self.half)]

    def copy(self, kind, side, i, ref, f, slot):
        c = self.chunk
        got = self.FIRST[kind] + slot[0] * self.PER_SIDE[kind] + slot[1]
        return rcopy(ref, ref, self.ssem.at[c, kind], self.rsem.at[c, got], f)

    def push(self, kind, side, i, ref, f, slot):
        self.copy(kind, side, i, ref, f, slot).start()

    def arrived(self, kind, side, i, ref):
        self.copy(kind, side, i, ref, self.pp.right, (side, i)).wait_recv()

    def sent(self, kind, n):
        self.copy(kind, 0, 0, self.piece(0, n), self.pp.right, (0, 0)).wait_send()

    def z_own(self, kind, ref):
        pp = self.pp
        self.push(kind, 0, 0, ref, pp.inner, (0, pp.z))

        @pl.when(pp.w == 1)
        def _():
            self.push(kind, 1, 0, ref, pp.edge, (0, pp.z))

    def z_forward(self, kind, r, zb, ref):
        pp = self.pp

        @pl.when((pp.w == 1) & (r == 1))
        def _():
            self.push(kind, 0, r, ref, pp.inner, (0, zb))

        @pl.when((pp.w == 1) & (r >= 2))
        def _():
            self.push(kind, 1, r, ref, pp.edge, (0, zb))

    def start(self):
        pp, c = self.pp, self.chunk
        self.z_own(0, self.piece(rows_a(c, pp.x, pp.z), RA))
        for side, f in ((0, pp.right), (1, pp.left)):
            self.push(3, side, 0, self.piece(rows_b(c, pp.x, pp.z), RB), f, (side, 0))

    def step(self, t):
        pp, c = self.pp, self.chunk
        z = pp.z
        sides = ((0, -1, pp.right), (1, 1, pp.left))
        zt, zl = pp.zb(t), pp.zb(t - 1)

        @pl.when((t >= 1) & (t <= 3))
        def _():
            ref = self.piece(rows_a(c, pp.x, zt), RA)
            self.arrived(0, 0, zt, ref)
            self.z_forward(0, t, zt, ref)

        @pl.when(t <= 3)
        def _():
            for side, _, f in sides:
                self.push(1, side, t, self.piece(rows_a(c, pp.x, zt), RA), f, (side, t))

        @pl.when(t == 0)
        def _():
            for side, dx, f in sides:
                start = rows_b(c, pp.col(dx), z)
                self.arrived(3, side, 0, self.piece(start, RB))
                self.push(4, side, 0, self.piece(start, RB, side), f, (side, 0))

        @pl.when((t >= 1) & (t <= 4))
        def _():
            for side, dx, f in sides:
                start = rows_a(c, pp.col(dx), zl)
                self.arrived(1, side, t - 1, self.piece(start, RA))
                self.push(2, side, t - 1, self.piece(start, RA, side), f, (side, t - 1))

        @pl.when(t == 1)
        def _():
            for side in (0, 1):
                self.arrived(4, side, 0, self.piece(rows_b(c, pp.col(2), z), RB, side))
            self.z_own(5, self.piece(rows_super(c, z), SUPER))

        @pl.when((t >= 2) & (t <= 4))
        def _():
            ref = self.piece(rows_super(c, zl), SUPER)
            self.arrived(5, 0, zl, ref)
            self.z_forward(5, t - 1, zl, ref)

        @pl.when(t >= 2)
        def _():
            zo = pp.zb(t - 2)
            for side in (0, 1):
                self.arrived(2, side, t - 2, self.piece(rows_a(c, pp.col(2), zo), RA, side))

    def work(self, t):
        pp, c = self.pp, self.chunk

        @pl.when((t >= 1) & (t <= 4))
        def _():
            self.compute(rows_super(c, pp.zb(t - 1)), SUPER)

        @pl.when(t >= 2)
        def _():
            self.compute(rows_line(c, pp.zb(t - 2)), LINE)

    def finish(self):
        for kind, n in ((0, RA), (5, SUPER)):

            @pl.when(self.pp.w == 0)
            def _():
                self.sent(kind, n)

            @pl.when(self.pp.w == 1)
            def _():
                self.sent(kind, 5 * n)

        for kind, n in ((1, 8 * RA), (2, 4 * RA), (3, 2 * RB), (4, RB)):
            self.sent(kind, n)


COLS = 512


def up(v):
    return v.astype(jnp.float32)


class Reduce:
    def __init__(self, pp, chunk, partial, sc):
        self.pp, self.chunk, self.partial, self.sc = pp, chunk, partial, sc
        self.width = sc.acc_a.shape[-1]

    def over(self, body, first=0, width=None):
        def run(k, carry):
            body(pl.ds(pl.multiple_of(first + k * COLS, 128), COLS))
            return carry

        lax.fori_loop(0, (width or self.width) // COLS, run, 0)

    FIRST = (0, 8, 16, 18, 23, 28)
    PER_SIDE = (4, 4, 1, 5, 5, 1)
    RECV = 30

    def copy(self, src, dst, kind, side, i, f, slot):
        c, sc = self.chunk, self.sc
        got = self.FIRST[kind] + slot[0] * self.PER_SIDE[kind] + slot[1]
        return rcopy(src, dst, sc.rs_send.at[c, kind], sc.rs_recv.at[c, got], f)

    def push(self, src, dst, kind, side, i, f, slot):
        self.copy(src, dst, kind, side, i, f, slot).start()

    def arrived(self, ref, kind, side, i):
        self.copy(ref, ref, kind, side, i, self.pp.right, (side, i)).wait_recv()

    def sent(self, ref, kind):
        self.copy(ref, ref, kind, 0, 0, self.pp.right, (0, 0)).wait_send()

    def z_stage(self, kind, r, acc, recv, send):
        pp, c, w = self.pp, self.chunk, self.pp.w

        @pl.when((w == 1) & (r >= 1))
        def _():
            self.arrived(recv.at[c, r], kind, 0, r)

            def add(cs):
                send[c, r - 1, :, cs] = (acc[c, :, cs] + up(recv[c, r, :, cs])).astype(jnp.bfloat16)

            self.over(add)

        @pl.when((w == 1) & (r >= 2))
        def _():
            slot = jnp.where(r == 3, 1, 0)
            self.push(send.at[c, r - 1], recv.at[c, slot], kind, 0, r, pp.inner, (0, slot))

        @pl.when((w == 1) & (r == 1))
        def _():
            self.push(send.at[c, r - 1], recv.at[c, 0], kind, 0, r, pp.edge, (0, 0))

        @pl.when((w == 0) & (r >= 1))
        def _():
            def cast(cs):
                send[c, r - 1, :, cs] = acc[c, :, cs].astype(jnp.bfloat16)

            self.over(cast)
            slot = jnp.where(r == 1, 4, r)
            self.push(send.at[c, r - 1], recv.at[c, slot], kind, 0, r, pp.inner, (0, slot))

        def last(i):
            self.arrived(recv.at[c, i], kind, 0, i)

            def add(cs):
                acc[c, :, cs] = acc[c, :, cs] + up(recv[c, i, :, cs])

            self.over(add)

        @pl.when(r == 0)
        def _():
            last(0)

        @pl.when((w == 1) & (r == 0))
        def _():
            last(4)

    def b_round(self, r):
        sc, c = self.sc, self.chunk
        start = rows_super(c, self.pp.zb(r))

        def fill(cs):
            sc.acc_b[c, :, cs] = self.partial(start, SUPER, cs)

        self.over(fill)
        self.z_stage(4, r, sc.acc_b, sc.b_recv, sc.b_send)

    def fill(self, r):
        sc, c = self.sc, self.chunk
        start = rows_line(c, self.pp.zb(r))

        def body(cs):
            sc.part[c, r, :, cs] = self.partial(start, LINE, cs).astype(jnp.bfloat16)

        self.over(body)

    def start(self):
        self.fill(3)

    def work(self, t):
        @pl.when(t <= 2)
        def _():
            self.fill(2 - t)

    def step(self, t):
        pp, sc, c, w = self.pp, self.sc, self.chunk, self.pp.w
        r0, r1, r2 = 3 - t, 4 - t, 5 - t
        half = self.width // 2

        def rows(dx, n):
            return pl.ds(pl.multiple_of(pp.col(dx) * n, 16), n)

        sides = ((0, 1, pp.right, half), (1, -1, pp.left, 0))

        @pl.when(t <= 3)
        def _():
            for side, _, f, lo in sides:
                src = sc.part.at[c, r0, rows(2, RA), pl.ds(lo, half)]
                self.push(src, sc.h_recv.at[c, side, r0], 0, side, r0, f, (side, r0))

        @pl.when((t == 0) & (w == 0))
        def _():
            def run(i, carry):
                self.b_round(3 - i)
                return carry

            lax.fori_loop(0, 3, run, 0)

        @pl.when((t >= 1) & (t <= 4))
        def _():
            for side, dx, f, lo in sides:
                self.arrived(sc.h_recv.at[c, side, r1], 0, side, r1)
                where = rows(dx, RA)

                def add(cs):
                    to = pl.ds(pl.multiple_of(lo + cs.start, 128), COLS)
                    sc.part[c, r1, where, to] = (up(sc.part[c, r1, where, to]) + up(sc.h_recv[c, side, r1, :, cs])).astype(jnp.bfloat16)

                self.over(add, width=half)
                self.push(sc.part.at[c, r1, where], sc.f_recv.at[c, side, r1], 1, side, r1, f, (side, r1))

        @pl.when((t >= 1) & (t <= 3) & (w == 1))
        def _():
            self.b_round(r1)

        @pl.when(t == 4)
        def _():
            self.b_round(0)
            sc.bh_send[c] = sc.acc_b[c, rows(2, RB), :].astype(jnp.bfloat16)
            for side, _, f, lo in sides:
                self.push(sc.bh_send.at[c, :, pl.ds(lo, half)], sc.bh_recv.at[c, side], 2, side, 0, f, (side, 0))

        @pl.when(t >= 2)
        def _():
            for side in (0, 1):
                self.arrived(sc.f_recv.at[c, side, r2], 1, side, r2)
            where = rows(0, RA)

            def fill(cs):
                sc.acc_a[c, :, cs] = up(sc.part[c, r2, where, cs]) + up(sc.f_recv[c, 0, r2, :, cs]) + up(sc.f_recv[c, 1, r2, :, cs])

            self.over(fill)
            self.z_stage(3, r2, sc.acc_a, sc.a_recv, sc.a_send)

        @pl.when(t == 4)
        def _():
            for side, dx, f, lo in sides:
                self.arrived(sc.bh_recv.at[c, side], 2, side, 0)
                where = rows(dx, RB)
                got, alone = pl.ds(lo, half), pl.ds(half - lo, half)
                sc.bf_send[c, side, :, got] = (sc.acc_b[c, where, got] + up(sc.bh_recv[c, side])).astype(jnp.bfloat16)
                sc.bf_send[c, side, :, alone] = sc.acc_b[c, where, alone].astype(jnp.bfloat16)
                self.push(sc.bf_send.at[c, side], sc.bf_recv.at[c, side], 5, side, 0, f, (side, 0))

    def finish(self):
        pp, sc, c = self.pp, self.sc, self.chunk
        for side in (0, 1):
            self.arrived(sc.bf_recv.at[c, side], 5, side, 0)
        own = pl.multiple_of(pp.x * RB, 16)
        sc.fin_b[...] = sc.acc_b[c, pl.ds(own, RB), :] + up(sc.bf_recv[c, 0]) + up(sc.bf_recv[c, 1])

    def drain(self):
        sc, c = self.sc, self.chunk
        sent = ((sc.h_recv, 0), (sc.f_recv, 1), (sc.bh_recv, 2), (sc.a_send, 3), (sc.b_send, 4), (sc.bf_recv, 5))
        for ref, kind in sent:
            self.sent(ref.at[c], kind)


class Refs:
    def __init__(self, **kw):
        self.__dict__.update(kw)


def scratch(width, hidden, modules, rows):
    bf, f32 = jnp.bfloat16, jnp.float32
    tokens = CHUNKS * CHUNK
    v = pltpu.VMEM
    return dict(
        xg=v((tokens, width), bf),
        og=v((tokens, width), bf),
        w_in=v((hidden, width), bf),
        w_out=v((hidden, width), bf),
        act=v((tokens, hidden), bf),
        slope=v((tokens, hidden), f32),
        pre_grad=v((tokens, hidden), bf),
        tgt=v((CHUNKS * OWN, width), bf),
        keep=v((CHUNKS * OWN, CHUNKS * OWN), f32),
        part=v((CHUNKS, 4, LINE, width), bf),
        h_recv=v((CHUNKS, 2, 4, RA, width // 2), bf),
        f_recv=v((CHUNKS, 2, 4, RA, width), bf),
        a_send=v((CHUNKS, 3, RA, width), bf),
        a_recv=v((CHUNKS, 5, RA, width), bf),
        b_send=v((CHUNKS, 3, SUPER, width), bf),
        b_recv=v((CHUNKS, 5, SUPER, width), bf),
        bh_send=v((CHUNKS, RB, width), bf),
        bh_recv=v((CHUNKS, 2, RB, width // 2), bf),
        bf_send=v((CHUNKS, 2, RB, width), bf),
        bf_recv=v((CHUNKS, 2, RB, width), bf),
        acc_a=v((CHUNKS, RA, width), f32),
        acc_b=v((CHUNKS, SUPER, width), f32),
        fin_b=v((RB, width), f32),
        g_send=pltpu.SemaphoreType.DMA((CHUNKS, 6)),
        g_recv=pltpu.SemaphoreType.DMA((CHUNKS, Gather.RECV)),
        rs_send=pltpu.SemaphoreType.DMA((CHUNKS, 6)),
        rs_recv=pltpu.SemaphoreType.DMA((CHUNKS, Reduce.RECV)),
        local=pltpu.SemaphoreType.DMA((5,)),
        own=pltpu.SemaphoreType.DMA((CHUNKS, 2)),
        d_send=v((2, 2, HALF, hidden, rows), bf),
        d_recv=v((2, 2, HALF, hidden, rows), bf),
        z_send=v((2, modules, hidden, rows), bf),
        z_recv=v((2, modules, hidden, rows), bf),
        fresh=v((2, modules, hidden, rows), bf),
        far_00=v((modules, SPLIT, rows), bf),
        far_01=v((modules, hidden - SPLIT, rows), bf),
        far_10=v((modules, SPLIT, rows), bf),
        far_11=v((modules, hidden - SPLIT, rows), bf),
        mast=v((2, modules, hidden, rows), f32),
        mom=v((2, modules, hidden, rows), f32),
        ds=pltpu.SemaphoreType.DMA((2, 2, PIECES)),
        dr=pltpu.SemaphoreType.DMA((2, 2, PIECES)),
        os=pltpu.SemaphoreType.DMA((2, 2, PIECES)),
        orv=pltpu.SemaphoreType.DMA((2, 2, PIECES)),
        own_out=pltpu.SemaphoreType.DMA((2, 2, PIECES)),
        zs=pltpu.SemaphoreType.DMA((2, 2, PIECES)),
        zr=pltpu.SemaphoreType.DMA((2, 2, PIECES)),
        out=pltpu.SemaphoreType.DMA((2, 2, PIECES)),
    )


HALF = 8
SPLIT = 128
PIECES = 2
PATHS_PER_MODULE = 4


class Group:
    def __init__(self):
        p = lax.axis_index("path")
        self.h, self.i = p // HALF, p % HALF
        self.y, self.c = self.i // 2, self.i % 2
        self.across = (1 - self.h) * HALF + self.i

    def peer(self, i):
        return self.h * HALF + i


def pcopy(src, dst, ssem, rsem, p):
    return pltpu.make_async_remote_copy(
        src_ref=src, dst_ref=dst, send_sem=ssem, recv_sem=rsem, device_id={"path": p}, device_id_type=MESH
    )


def path_phase(pg, sc, width_scale, hidden_scale, table, new_w, new_mast, new_mom):
    h, me = pg.h, pg.i
    hidden, rows = sc.mast.shape[2:]
    modules = sc.mast.shape[1]
    operands = ((sc.xg, sc.pre_grad, width_scale), (sc.og, sc.act, hidden_scale))

    def half(side):
        return h if side == 0 else 1 - h

    STEP = 32
    pieces = ((0, SPLIT), (SPLIT, hidden - SPLIT))

    def units(piece):
        return pl.ds(*pieces[piece])

    def dcopy(level, side, piece, i, src):
        return pcopy(
            sc.d_send.at[level, side, i, units(piece)],
            sc.d_recv.at[level, side, src, units(piece)],
            sc.ds.at[level, side, piece],
            sc.dr.at[level, side, piece],
            pg.peer(i),
        )

    def changes(level, side, which):
        left, right, scale = operands[level]
        first = pieces[which[0]][0]
        count = sum(pieces[piece][1] for piece in which)

        def run(k, c):
            d = jnp.where(k == 0, 2, jnp.where(k == 1, 1, jnp.where(k == 2, 3, 0)))
            y = (pg.y + d) % 4
            cols = pl.ds(pl.multiple_of((half(side) * HALF + 2 * y) * rows, 128), 2 * rows)
            g = lax.dot_general(
                right[:, first : first + count], left[:, cols], (((0,), (0,)), ((), ())), preferred_element_type=jnp.float32
            )
            g = (INNER_LR * scale * g).astype(jnp.bfloat16)
            for core in (0, 1):
                i = 2 * y + core
                part = g[:, core * rows : (core + 1) * rows]

                @pl.when(i == me)
                def _():
                    sc.d_recv[level, side, i, pl.ds(first, count), :] = part

                @pl.when(i != me)
                def _():
                    sc.d_send[level, side, i, pl.ds(first, count), :] = part
                    for piece in which:
                        dcopy(level, side, piece, i, me).start()

            return c

        lax.fori_loop(0, 4, run, 0)

    def all_dcopies(level, side, piece):
        ref = sc.d_recv.at[level, side, pl.ds(0, HALF - 1), units(piece)]
        return pcopy(ref, ref, sc.ds.at[level, side, piece], sc.dr.at[level, side, piece], pg.across)

    def await_changes(level, side, piece):
        all_dcopies(level, side, piece).wait_recv()

    def sums(level, side, piece, use):
        def run(k, c):
            part = pl.ds(pl.multiple_of(pieces[piece][0] + k * STEP, STEP), STEP)
            total = [jnp.zeros((STEP, rows), jnp.float32) for _ in range(modules)]
            for i in range(HALF):
                change = sc.d_recv[level, side, i, part, :].astype(jnp.float32)
                named = table[level, pg.peer(i)]
                for m in range(modules):
                    total[m] = total[m] + jnp.where(named == m, 1.0, 0.0) * change
            for m in range(modules):
                use(m, part, total[m])
            return c

        lax.fori_loop(0, pieces[piece][1] // STEP, run, 0)

    far = ((sc.far_00, sc.far_01), (sc.far_10, sc.far_11))

    def zcopy(kind, level, piece):
        src = (sc.z_send, sc.fresh)[kind].at[level, :, units(piece)]
        dst = far[level][piece] if kind else sc.z_recv.at[level, :, units(piece)]
        return pcopy(src, dst, sc.zs.at[kind, level, piece], sc.zr.at[kind, level, piece], pg.across)

    def sums_across(level, piece):
        await_changes(level, 1, piece)

        def use(m, part, total):
            sc.z_send[level, m, part, :] = total.astype(jnp.bfloat16)

        sums(level, 1, piece, use)
        zcopy(0, level, piece).start()

    def outs(level, piece):
        where = (level, slice(None), units(piece))
        return [
            pltpu.make_async_copy(sc.mast.at[where], new_mast.at[where], sc.out.at[0, level, piece]),
            pltpu.make_async_copy(sc.mom.at[where], new_mom.at[where], sc.out.at[1, level, piece]),
        ]

    def update(level, piece):
        await_changes(level, 0, piece)
        zcopy(0, level, piece).wait_recv()

        def use(m, part, total):
            average = (total + sc.z_recv[level, m, part, :].astype(jnp.float32)) * (1.0 / PATHS_PER_MODULE)
            moved = MOMENT * sc.mom[level, m, part, :] + average
            master = sc.mast[level, m, part, :] - OUTER_LR * (average + MOMENT * moved)
            sc.mom[level, m, part, :] = moved
            sc.mast[level, m, part, :] = master
            sc.fresh[level, m, part, :] = master.astype(jnp.bfloat16)

        sums(level, 0, piece, use)
        if (level, piece) != (0, 0):
            zcopy(1, level, piece).start()
        for c in outs(level, piece):
            c.start()

    def ocopy(level, side, piece, i, src):
        place = pl.ds(pl.multiple_of((half(side) * HALF + src) * rows, 128), rows)
        return pcopy(
            sc.d_send.at[level, side, i, units(piece)],
            new_w.at[level, units(piece), place],
            sc.os.at[level, side, piece],
            sc.orv.at[level, side, piece],
            pg.peer(i),
        )

    def own_copy(level, side, piece):
        place = pl.ds(pl.multiple_of((half(side) * HALF + me) * rows, 128), rows)
        return pltpu.make_async_copy(
            sc.d_send.at[level, side, me, units(piece)],
            new_w.at[level, units(piece), place],
            sc.own_out.at[level, side, piece],
        )

    def hand_back(level, side, piece):
        if side == 1:
            zcopy(1, level, piece).wait_recv()
        all_dcopies(level, side, piece).wait_send()

        def run(k, c):
            i = (me + 1 + k) % HALF
            named = table[level, pg.peer(i)]
            new = sc.fresh[level, named, units(piece), :] if side == 0 else far[level][piece][named]
            sc.d_send[level, side, i, units(piece), :] = new

            @pl.when(i != me)
            def _():
                ocopy(level, side, piece, i, me).start()

            @pl.when(i == me)
            def _():
                own_copy(level, side, piece).start()

            return c

        lax.fori_loop(0, HALF, run, 0)

    changes(1, 1, (0,))
    changes(1, 1, (1,))
    sums_across(1, 0)
    changes(1, 0, (0, 1))
    sums_across(1, 1)
    changes(0, 1, (1,))
    changes(0, 1, (0,))
    update(1, 0)
    sums_across(0, 1)
    sums_across(0, 0)
    update(1, 1)
    changes(0, 0, (0, 1))
    hand_back(1, 0, 0)
    hand_back(1, 0, 1)
    update(0, 1)
    update(0, 0)
    hand_back(1, 1, 0)
    hand_back(0, 0, 1)
    hand_back(0, 0, 0)
    hand_back(1, 1, 1)
    zcopy(1, 0, 1).wait_send()
    zcopy(1, 0, 0).start()
    hand_back(0, 1, 1)
    hand_back(0, 1, 0)

    for level in (0, 1):
        for side in (0, 1):
            for piece in range(PIECES):
                own_copy(level, side, piece).wait()
                ref = sc.d_send.at[level, side, pl.ds(0, HALF - 1), units(piece)]
                others = pcopy(ref, ref, sc.os.at[level, side, piece], sc.orv.at[level, side, piece], pg.across)
                others.wait_recv()
                others.wait_send()
        for piece in range(PIECES):
            zcopy(0, level, piece).wait_send()
            if (level, piece) != (0, 1):
                zcopy(1, level, piece).wait_send()
            for c in outs(level, piece):
                c.wait()


def step_kernel(names, width_scale, hidden_scale, tokens, x_ref, t_ref, ids_ref, table_ref, w_ref, mast_ref, mom_ref,
                new_w_ref, new_mast_ref, new_mom_ref, *refs):
    sc = Refs(**dict(zip(names, refs)))
    pp = Place()
    pg = Group()
    x, z, w = pp.x, pp.z, pp.w
    own = [(c * OWN, rows_a(c, x, z), RA) for c in range(CHUNKS)] + [(c * OWN + RA, rows_b(c, x, z), RB) for c in range(CHUNKS)]

    mine = [
        pltpu.make_async_copy(x_ref.at[pl.ds(lo, n)], sc.xg.at[pl.ds(start, n)], sc.own.at[k // 2, k % 2])
        for k, (lo, start, n) in enumerate(own)
    ]
    loads = [
        pltpu.make_async_copy(w_ref.at[0], sc.w_in, sc.local.at[0]),
        pltpu.make_async_copy(w_ref.at[1], sc.w_out, sc.local.at[1]),
        pltpu.make_async_copy(t_ref, sc.tgt, sc.local.at[2]),
        pltpu.make_async_copy(mast_ref, sc.mast, sc.local.at[3]),
        pltpu.make_async_copy(mom_ref, sc.mom, sc.local.at[4]),
    ]
    for c in mine + loads:
        c.start()

    barrier = pltpu.get_barrier_semaphore()
    for f in (pp.right, pp.left, pp.inner):
        pl.semaphore_signal(barrier, inc=1, device_id={"fsdp": f}, device_id_type=MESH)

    @pl.when(w == 1)
    def _():
        pl.semaphore_signal(barrier, inc=1, device_id={"fsdp": pp.edge}, device_id_type=MESH)

    for i in range(HALF):

        @pl.when(pg.i != i)
        def _():
            pl.semaphore_signal(barrier, inc=1, device_id={"path": pg.peer(i)}, device_id_type=MESH)

    pl.semaphore_signal(barrier, inc=1, device_id={"path": pg.across}, device_id_type=MESH)
    pl.semaphore_wait(barrier, 3 + HALF + w)
    for c in mine + loads[:1]:
        c.wait()

    def across_width(rows, weights):
        return lax.dot_general(rows, weights[...], (((1,), (1,)), ((), ())), preferred_element_type=jnp.float32)

    def forward(start, n):
        rows = pl.ds(start, n)
        pre = across_width(sc.xg[rows, :], sc.w_in) * width_scale
        sig = jax.nn.sigmoid(pre)
        sc.act[rows, :] = (pre * sig).astype(jnp.bfloat16)
        sc.slope[rows, :] = sig * (1.0 + pre * (1.0 - sig))

    def partial(start, n, cs):
        return jnp.dot(sc.act[pl.ds(start, n), :], sc.w_out[:, cs], preferred_element_type=jnp.float32) * hidden_scale

    def loss_grad(total, lo, start, n):
        res = up(sc.xg[pl.ds(start, n), :]) + total - up(sc.tgt[pl.ds(lo, n), :])
        sc.og[pl.ds(start, n), :] = (sc.keep[pl.ds(lo, n), 0:1] * res / tokens).astype(jnp.bfloat16)

    def backward(start, n):
        rows = pl.ds(start, n)
        act_grad = across_width(sc.og[rows, :], sc.w_out) * hidden_scale
        sc.pre_grad[rows, :] = (act_grad * sc.slope[rows, :]).astype(jnp.bfloat16)

    first = [Gather(pp, c, sc.xg, sc.g_send, sc.g_recv, forward) for c in range(CHUNKS)]
    sums = [Reduce(pp, c, partial, sc) for c in range(CHUNKS)]
    second = [Gather(pp, c, sc.og, sc.g_send, sc.g_recv, backward) for c in range(CHUNKS)]

    def turn_over(c):
        sums[c].finish()
        loss_grad(sc.acc_a[c], *own[c])
        loss_grad(sc.fin_b[...], *own[CHUNKS + c])
        first[c].finish()
        second[c].start()

    def steps(*jobs):
        def run(k, carry):
            for job, offset in jobs:
                job.step(k + offset)
            for job, offset in jobs:
                job.work(k + offset)
            return carry

        lax.fori_loop(0, STEPS // 2, run, 0)

    late = STEPS // 2
    first[0].start()
    steps((first[0], 0))
    first[1].start()
    steps((first[0], late), (first[1], 0))
    for c in loads[1:]:
        c.wait()
    kept = (ids_ref[...] >= SPECIAL).astype(jnp.float32)
    sc.keep[...] = jnp.broadcast_to(kept, sc.keep.shape).T
    sums[0].start()
    steps((sums[0], 0), (first[1], late))
    sums[1].start()
    steps((sums[0], late), (sums[1], 0))
    turn_over(0)
    steps((second[0], 0), (sums[1], late))
    turn_over(1)
    steps((second[0], late), (second[1], 0))
    steps((second[1], late))
    path_phase(pg, sc, width_scale, hidden_scale, table_ref, new_w_ref, new_mast_ref, new_mom_ref)
    for job in second:
        job.finish()
    for job in sums:
        job.drain()


LANES = 4


def land_kernel(*refs):
    count = (len(refs) - 2) // 3
    sems_in, sems_out = refs[-2:]
    ins, outs = [], []
    for k in range(count):
        src, dst, stage = refs[k], refs[count + k], refs[2 * count + k]
        size = src.shape[-2] // LANES // 16 * 16
        for lane in range(LANES):
            n = size if lane < LANES - 1 else src.shape[-2] - lane * size
            where = (slice(None),) * (len(src.shape) - 2) + (pl.ds(lane * size, n),)
            ins.append(pltpu.make_async_copy(src.at[where], stage.at[where], sems_in.at[k, lane]))
            outs.append(pltpu.make_async_copy(stage.at[where], dst.at[where], sems_out.at[k, lane]))
    for c in ins:
        c.start()
    for got, put in zip(ins, outs):
        got.wait()
        put.start()
    for c in outs:
        c.wait()


def land(*arrays):
    hbm = pl.BlockSpec(memory_space=pl.ANY)
    return pl.pallas_call(
        land_kernel,
        out_shape=tuple(jax.ShapeDtypeStruct(v.shape, v.dtype) for v in arrays),
        in_specs=[hbm] * len(arrays),
        out_specs=(hbm,) * len(arrays),
        scratch_shapes=[pltpu.VMEM(v.shape, v.dtype) for v in arrays] + [pltpu.SemaphoreType.DMA((len(arrays), LANES))] * 2,
        compiler_params=pltpu.CompilerParams(vmem_limit_bytes=60 * 1024 * 1024),
        name="land",
    )(*arrays)


def turn(v):
    return jnp.swapaxes(v, -1, -2)


def per_device(inputs, targets, token_ids, module_table, path_weights, master, momentum):
    width, hidden = path_weights.shape[2:]
    n = lax.axis_size("fsdp")
    tokens = inputs.shape[1] * n
    modules, rows = master.shape[1:3]
    spec = scratch(width, hidden, modules, rows)
    hbm = pl.BlockSpec(memory_space=pl.ANY)
    vmem = pl.BlockSpec(memory_space=pltpu.VMEM)
    smem = pl.BlockSpec(memory_space=pltpu.SMEM)
    new_weights, new_master, new_momentum = pl.pallas_call(
        functools.partial(step_kernel, tuple(spec), width ** (-0.5), (hidden * n) ** (-0.5), tokens),
        out_shape=(
            jax.ShapeDtypeStruct((2, hidden, width), jnp.bfloat16),
            jax.ShapeDtypeStruct((2, modules, hidden, rows), jnp.float32),
            jax.ShapeDtypeStruct((2, modules, hidden, rows), jnp.float32),
        ),
        in_specs=[hbm, hbm, vmem, smem, hbm, hbm, hbm],
        out_specs=(hbm, hbm, hbm),
        scratch_shapes=list(spec.values()),
        compiler_params=pltpu.CompilerParams(
            collective_id=0, has_side_effects=True, vmem_limit_bytes=63 * 1024 * 1024
        ),
        name="outer_step",
    )(inputs[0], targets[0], token_ids, module_table.T, turn(path_weights[0]), turn(master), turn(momentum))
    new_weights, new_master, new_momentum = land(new_weights, new_master, new_momentum)
    return (turn(new_weights)[None], turn(new_master), turn(new_momentum))


def solution(mesh):
    in_specs = (
        P("path", "fsdp", None),
        P("path", "fsdp", None),
        P("path", "fsdp"),
        P(),
        P("path", None, None, "fsdp"),
        P(None, None, "path", "fsdp"),
        P(None, None, "path", "fsdp"),
    )
    out_specs = (
        P("path", None, None, "fsdp"),
        P(None, None, "path", "fsdp"),
        P(None, None, "path", "fsdp"),
    )
    return jax.shard_map(
        per_device, mesh=mesh, in_specs=in_specs, out_specs=out_specs, check_vma=False
    )
```
